256 devices in a mesh: coil: 8 (over x, core), tile: 32 (over z, y).
Axes of the slice: x: 4, y: 4, z: 8, core: 2. Of those that a mesh axis runs over, the one named last changes fastest.
Arguments:
- image_p: float32 [2, 128, 128, 128], P(None, 'tile', 'coil'), may hold values from -6 to 6
- image_x: float32 [2, 128, 128, 128], P(None, 'tile', 'coil'), may hold values from -6 to 6
- image_r: float32 [2, 128, 128, 128], P(None, 'tile', 'coil'), may hold values from -6 to 6
- sensitivity: float32 [8, 2, 128, 128, 128], P('coil', None, 'tile'), may hold values from -5 to 5
- kb_weights: float32 [1024, 3, 4, 128], P('tile'), may hold values from -3 to 3
- block_owner: int32 [1024], P('tile'), may hold values from 0 to 31, as said below
- owner_list: int32 [3, 32, 32, 4], P(None, 'tile'), may hold values from -1 to 124, as said below
Outputs:
- next_x: float32 [2, 128, 128, 128], P(None, 'tile', 'coil')
- next_r: float32 [2, 128, 128, 128], P(None, 'tile', 'coil')
- next_p: float32 [2, 128, 128, 128], P(None, 'tile', 'coil')
The draws below stay inside these ranges and needn't reach their ends.
Inputs may be any that keep to these rules, and one draw needn't show every extreme that they name: `block_owner`: of the 32 blocks handled by one index of tile (blocks h * 32 to h * 32 + 31), at most 4 have any one owner; in every draw each such device has exactly 4 blocks of one common owner. owner_list[:, o, h, k] holds the offsets (kx, ky within tile o, kz) of the block of rank k among the blocks of device h whose owner is o, in the order of their slots; all three are -1 where there is no such block. Offsets place the whole box inside the grid and inside tile o.
All inputs are finite; a program needn't handle non-finite values.
Results may differ from the reference program's by a relative error of at most 0.0002.
Values sent between devices are 32-bit elements; how exact they have to be, the bound alone decides.
A program may use at most 128 MiB of HBM per device.

```python
import jax
import jax.numpy as jnp
from jax import lax

GRID = 128
COILS = 8
BOX = 4
BSAMP = 128
SLOTS = 32
BLOCKS = 1024
CAP = 4
N_TILE = 32


def routing(key):
    key = jax.random.fold_in(key, 11)
    key_hot, key_shift, key_perm, key_x, key_y, key_z = jax.random.split(key, 6)
    hot = N_TILE // 4 + jax.random.randint(key_hot, (), 0, N_TILE // 2)
    index = jnp.arange(SLOTS, dtype=jnp.int32)
    shifts = jax.random.randint(key_shift, (N_TILE,), 0, N_TILE)
    spread = (hot + 1 + (index[None, :] + shifts[:, None]) % (N_TILE - 1)) % N_TILE
    base = jnp.where(index[None, :] < CAP, hot, spread).astype(jnp.int32)
    perms = jax.vmap(lambda k: jax.random.permutation(k, SLOTS))(jax.random.split(key_perm, N_TILE))
    owners = jnp.take_along_axis(base, perms, axis=1).astype(jnp.int32)
    onehot = (owners[:, :, None] == jnp.arange(N_TILE, dtype=jnp.int32)[None, None, :]).astype(jnp.int32)
    ranks = jnp.sum((jnp.cumsum(onehot, axis=1) - onehot) * onehot, axis=2)
    span = GRID - BOX + 1
    inner = GRID // N_TILE - BOX + 1
    off_x = jax.random.randint(key_x, (N_TILE, SLOTS), 0, span)
    off_y = jax.random.randint(key_y, (N_TILE, SLOTS), 0, inner)
    off_z = jax.random.randint(key_z, (N_TILE, SLOTS), 0, span)
    off_x = off_x.at[:, 0].set(GRID - BOX).at[:, 1].set(0)
    off_y = off_y.at[:, 0].set(GRID // N_TILE - BOX).at[:, 1].set(0)
    off_z = off_z.at[:, 0].set(GRID - BOX).at[:, 1].set(0)
    offsets = jnp.stack([off_x, off_y, off_z]).astype(jnp.int32)
    helpers = jnp.broadcast_to(jnp.arange(N_TILE, dtype=jnp.int32)[:, None], owners.shape)
    lists = jnp.full((3, N_TILE, N_TILE, CAP), -1, jnp.int32)
    lists = lists.at[:, owners, helpers, ranks].set(offsets)
    return (owners.reshape(-1), lists)


def draw_block_owner(key, part):
    return routing(key)[0]


def draw_owner_list(key, part):
    return routing(key)[1]


def block_levels(stream_key, shape, pieces, smallest, high):
    loudness = 1.0
    for axis_at, shards_of in pieces:
        draws = jax.random.uniform(jax.random.fold_in(jax.random.fold_in(stream_key, 6), axis_at), (shards_of,), jnp.float32, smallest / len(pieces), high / len(pieces))
        loudness = loudness * jnp.repeat(jnp.exp(draws), shape[axis_at] // shards_of).reshape((-1,) + (1,) * (len(shape) - 1 - axis_at))
    return loudness


def scatter_about(rng, dims, scale, limit, pieces=(), held_as=jnp.bfloat16):
    values = jax.random.normal(rng, dims, jnp.float32) * scale
    if len(pieces) > 0:
        values = block_levels(rng, dims, pieces, -0.22, 0.18) * values
    return jnp.clip(values, min=-limit, max=limit).astype(held_as)


def setup_inputs(seed: int = 0) -> dict:
    splits = jax.random.split(jax.random.key(seed), 8)
    return {
        "image_p": scatter_about(splits[0], (2, GRID, GRID, GRID), 1.0, 6.0, ((1, 32), (2, 8)), jnp.float32),
        "image_x": scatter_about(splits[1], (2, GRID, GRID, GRID), 1.0, 6.0, ((1, 32), (2, 8)), jnp.float32),
        "image_r": scatter_about(splits[2], (2, GRID, GRID, GRID), 1.0, 6.0, ((1, 32), (2, 8)), jnp.float32),
        "sensitivity": scatter_about(splits[3], (COILS, 2, GRID, GRID, GRID), 0.35, 5.0, ((0, 8), (2, 32)), jnp.float32),
        "kb_weights": scatter_about(splits[4], (BLOCKS, 3, BOX, BSAMP), BOX ** -0.5, 3.0, ((0, 32),), jnp.float32),
        "block_owner": draw_block_owner(jax.random.fold_in(splits[7], 71), 0),
        "owner_list": draw_owner_list(jax.random.fold_in(splits[7], 71), 0),
    }


def regrid(boxes, weights):
    count = boxes.shape[0]
    width = weights.shape[2]
    cube = boxes.reshape(count, 2, width, width, width)
    w_x = weights[:, 0]
    w_y = weights[:, 1]
    w_z = weights[:, 2]
    values = jnp.einsum("ncijk,nis,njs,nks->ncs", cube, w_x, w_y, w_z, precision=lax.Precision.HIGHEST)
    back = jnp.einsum("ncs,nis,njs,nks->ncijk", values, w_x, w_y, w_z, precision=lax.Precision.HIGHEST)
    return back.reshape(count, -1)


def regrid_groups(boxes, weights, group):
    count = boxes.shape[0]
    grouped = (boxes.reshape(count // group, group, boxes.shape[1]), weights.reshape((count // group, group) + weights.shape[1:]))
    done = lax.map(lambda pair: regrid(pair[0], pair[1]), grouped)
    return done.reshape(count, -1)


def cut_box(field, off_x, off_y, off_z, width):
    start = (jnp.zeros((), jnp.int32), off_x, off_y, off_z)
    return lax.dynamic_slice(field, start, (2, width, width, width))


def place_boxes(grid, boxes, off_x, off_y, off_z, width):
    count = boxes.shape[0]
    cells = jnp.arange(width, dtype=jnp.int32)
    index_x = off_x[:, None, None, None] + cells[None, :, None, None]
    index_y = off_y[:, None, None, None] + cells[None, None, :, None]
    index_z = off_z[:, None, None, None] + cells[None, None, None, :]
    values = jnp.transpose(boxes.reshape(count, 2, width, width, width), (1, 0, 2, 3, 4))
    return grid.at[:, index_x, index_y, index_z].add(values)


def ranks_of(owners, ntile):
    onehot = (owners[:, :, None] == jnp.arange(ntile, dtype=jnp.int32)[None, None, :]).astype(jnp.int32)
    return jnp.sum((jnp.cumsum(onehot, axis=1) - onehot) * onehot, axis=2)


def reference(image_p, image_x, image_r, sensitivity, kb_weights, block_owner, owner_list):
    width = BOX
    owners = block_owner.reshape(N_TILE, SLOTS)
    ranks = ranks_of(owners, N_TILE)
    helpers = jnp.broadcast_to(jnp.arange(N_TILE, dtype=jnp.int32)[:, None], owners.shape)
    offsets = owner_list[:, owners, helpers, ranks].reshape(3, -1).astype(jnp.int32)
    off_x = offsets[0]
    off_y = offsets[1] + block_owner.astype(jnp.int32) * (GRID // N_TILE)
    off_z = offsets[2]
    direction = lax.complex(image_p[0], image_p[1])

    def one_coil(total, sens):
        smap = lax.complex(sens[0], sens[1])
        kspace = jnp.fft.fftn(smap * direction, norm="ortho")
        kstack = jnp.stack([jnp.real(kspace), jnp.imag(kspace)])
        boxes = jax.vmap(cut_box, in_axes=(None, 0, 0, 0, None))(kstack, off_x, off_y, off_z, width)
        boxes = boxes.reshape(boxes.shape[0], -1)
        done = regrid_groups(boxes, kb_weights, SLOTS)
        gridded = place_boxes(jnp.zeros_like(kstack), done, off_x, off_y, off_z, width)
        image = jnp.fft.ifftn(lax.complex(gridded[0], gridded[1]), norm="ortho")
        back = jnp.conj(smap) * image
        return total + jnp.stack([jnp.real(back), jnp.imag(back)]), None

    normal, unused = lax.scan(one_coil, jnp.zeros_like(image_p), sensitivity)
    norm_now = jnp.sum(image_r * image_r)
    alpha = norm_now / jnp.sum(image_p * normal)
    next_x = image_x + alpha * image_p
    next_r = image_r - alpha * normal
    norm_next = jnp.sum(next_r * next_r)
    next_p = next_r + (norm_next / norm_now) * image_p
    return next_x, next_r, next_p
```

```python
import functools
import math

import jax
import jax.numpy as jnp
import ml_dtypes
import numpy as np
from jax import lax
from jax.experimental import pallas as pl
from jax.experimental.pallas import tpu as pltpu
from jax.sharding import PartitionSpec as P

N = 128
NC = 8
NT = 32
CAP = 4
SLOTS = 32
F32, BF16, I32 = jnp.float32, jnp.bfloat16, jnp.int32
MESH = pl.DeviceIdType.MESH
ANY = pl.BlockSpec(memory_space=pl.ANY)
SMEM = pl.BlockSpec(memory_space=pltpu.SMEM)


def tables():
    cells = np.arange(N)
    angle = 2.0 * math.pi / N * ((cells[:, None] * cells[None, :]) % N)
    cos, sin = np.cos(angle) / math.sqrt(N), np.sin(angle) / math.sqrt(N)
    left = np.block([[cos, sin], [-sin, cos]])
    order = [c * N + 4 * t + i for t in range(NT) for c in range(2) for i in range(4)]
    out = []
    for table in (left, left.T, left[:, order], left[:, order].T):
        table = table.astype(np.float32)
        high = table.astype(ml_dtypes.bfloat16)
        low = (table - high.astype(np.float32)).astype(ml_dtypes.bfloat16)
        out += [high, low]
    return np.stack(out)


def split(x):
    high = x.astype(BF16)
    return high, (x - high.astype(F32)).astype(BF16)


def dot(a, b):
    return jnp.dot(a, b, preferred_element_type=F32)


def dot3(a, b):
    return dot(a[0], b[0]) + (dot(a[0], b[1]) + dot(a[1], b[0]))


def kernel(
    p_hbm, x_hbm, r_hbm, s_hbm, kb_hbm, own, offs, tab_hbm,
    ox_hbm, or_hbm, op_hbm,
    tab, smap, kb, xv, rv, pbuf, wsend, wbuf, onehot, pt, pi,
    send1, recv1, boxes, placed, gacc, send2, recv2, rs_send, rs_recv,
    nx, nr, npv, ar1, ar1c, ar1t, ar2, ar2c, ar2t,
    load_sem, loc_sem, ag_s, ag_r, w1_s, w1_r, w2_s, w2_r, a1_s, a1_r, a2_s, a2_r,
    rs_s, rs_r, r1c_s, r1c_r, r1t_s, r1t_r, r2c_s, r2c_r, r2t_s, r2t_r, out_sem,
):
    ci, ti = lax.axis_index("coil"), lax.axis_index("tile")

    loads = [
        pltpu.make_async_copy(src, dst, load_sem.at[i])
        for i, (src, dst) in enumerate(
            [
                (kb_hbm, kb),
                (tab_hbm, tab),
                (s_hbm.at[0], smap),
                (p_hbm, pbuf.at[ci]),
                (x_hbm, xv),
                (r_hbm, rv),
            ]
        )
    ]
    for load in loads:
        load.start()

    def others(size, me, body):
        def step(s, carry):
            body(lax.rem(me + s, size))
            return carry

        lax.fori_loop(1, size, step, 0)

    barrier = pltpu.get_barrier_semaphore()
    others(NT, ti, lambda t: pl.semaphore_signal(barrier, inc=1, device_id=(ci, t), device_id_type=MESH))
    others(NC, ci, lambda c: pl.semaphore_signal(barrier, inc=1, device_id=(c, ti), device_id_type=MESH))

    def push(src, dst, sems, device):
        pltpu.make_async_remote_copy(
            src_ref=src, dst_ref=dst, send_sem=sems[0], recv_sem=sems[1],
            device_id=device, device_id_type=MESH,
        ).start()

    def await_bytes(ref, sem):
        pltpu.make_async_copy(ref, ref, sem).wait()

    sub = lax.broadcasted_iota(I32, (NT, N), 0)
    lane = lax.broadcasted_iota(I32, (NT, N), 1)
    rank = ci // 2
    count = jnp.zeros((NT, N), I32)
    pick = jnp.zeros((NT, N), F32)
    for j in range(SLOTS):
        mine = sub == own[j]
        pick = jnp.where(mine & (lane == j) & (count == rank), 1.0, pick)
        count = jnp.where(mine, count + 1, count)
    pick = pick[:, :SLOTS].astype(BF16)
    loads[0].wait()
    first = lax.rem(ci, 2) == 0
    for i in range(8):
        row_a = kb[pl.ds(i // 2, SLOTS, stride=12), :]
        row_b = kb[pl.ds(4 + i, SLOTS, stride=12), :]
        row = jnp.where(first, row_a, row_b)
        high, rest = split(row)
        mid, low = split(row - high.astype(F32))
        del rest
        wsend[pl.ds(i, NT, stride=8), :] = dot(pick, high) + (dot(pick, mid) + dot(pick, low))

    pl.semaphore_wait(barrier, NT - 1 + NC - 1)

    others(NC, ci, lambda c: push(p_hbm, pbuf.at[ci], (ag_s, ag_r), (c, ti)))
    others(NT, ti, lambda t: push(
        wsend.at[pl.ds(pl.multiple_of(t * 8, 8), 8)], wbuf.at[ci, ti], (w1_s, w1_r), (ci, t)))
    own_w = pltpu.make_async_copy(wsend.at[pl.ds(pl.multiple_of(ti * 8, 8), 8)], wbuf.at[ci, ti], loc_sem.at[0])
    own_w.start()

    sub16 = lax.broadcasted_iota(I32, (16, 2 * N), 0)
    lane16 = lax.broadcasted_iota(I32, (16, 2 * N), 1)
    base16 = (sub16 & 1) * N + ((sub16 >> 1) & 3)

    def mark(h, carry):
        for half in range(2):
            start = jnp.where(sub16 < 8, offs[0, 0, h, 2 * half], offs[0, 0, h, 2 * half + 1])
            hit = jnp.where(lane16 == base16 + start, 1.0, 0.0).astype(BF16)
            onehot[pl.ds(pl.multiple_of(h * 32 + half * 16, 16), 16), :] = hit
        return carry

    lax.fori_loop(0, NT, mark, 0)
    loads[1].wait()

    def phases(g, carry):
        rows = pl.ds(pl.multiple_of(g * 256, 256), 256)
        hot = onehot[rows, :]
        for i in range(2):
            pt[i, rows, :] = dot(hot, tab[4 + i]).astype(BF16)
            pi[i, g] = lax.dot_general(
                tab[6 + i], hot, (((1,), (1,)), ((), ())), preferred_element_type=F32
            ).astype(BF16)
        return carry

    lax.fori_loop(0, 4, phases, 0)

    loads[2].wait()
    loads[3].wait()
    await_bytes(pbuf.at[pl.ds(0, NC - 1)], ag_r)
    left, right = (tab[0], tab[1]), (tab[2], tab[3])
    for pair in range(2):
        parts = []
        for xi in (2 * pair, 2 * pair + 1):
            p_re = pbuf[:, 0, xi].reshape(N, N)
            p_im = pbuf[:, 1, xi].reshape(N, N)
            s_re, s_im = smap[0, xi], smap[1, xi]
            parts.append(jnp.concatenate([s_re * p_re - s_im * p_im, s_re * p_im + s_im * p_re], axis=1))
        along_z = dot3(split(jnp.concatenate(parts, axis=0)), right)
        columns = [
            jnp.concatenate([along_z[i * N : (i + 1) * N, :N], along_z[i * N : (i + 1) * N, N:]], axis=0)
            for i in range(2)
        ]
        along_y = dot3(left, split(jnp.concatenate(columns, axis=1)))
        for i in range(2):
            for c in range(2):
                send1[pl.ds(c * 4 + 2 * pair + i, N, stride=8), :] = along_y[
                    c * N : (c + 1) * N, i * N : (i + 1) * N
                ]

    def rows_of(t):
        return pl.ds(pl.multiple_of(t * 32, 32), 32)

    others(NT, ti, lambda t: push(send1.at[rows_of(t)], recv1.at[ti], (a1_s, a1_r), (ci, t)))
    own_1 = pltpu.make_async_copy(send1.at[rows_of(ti)], recv1.at[ti], loc_sem.at[1])
    own_1.start()

    own_w.wait()
    await_bytes(wbuf.at[ci, pl.ds(0, NT - 1)], w1_r)
    others(NC, ci, lambda c: push(wbuf.at[ci], wbuf.at[ci], (w2_s, w2_r), (c, ti)))

    loads[5].wait()
    norm_part = jnp.sum(rv[...].reshape(16, 8, N) * rv[...].reshape(16, 8, N), axis=0)

    own_1.wait()
    await_bytes(recv1.at[pl.ds(0, NT - 1)], a1_r)
    for e in range(0, 4, 2):
        got = [recv1[:, (e + i) * 8 : (e + i + 1) * 8, :].reshape(2 * N, N) for i in range(2)]
        field = split(jnp.concatenate(got, axis=1))

        def cut(g, carry, e=e, field=field):
            rows = pl.ds(pl.multiple_of(g * 256, 256), 256)
            boxes[rows, e * N : (e + 2) * N] = dot3((pt[0, rows, :], pt[1, rows, :]), field)
            return carry

        lax.fori_loop(0, 4, cut, 0)

    await_bytes(wbuf.at[pl.ds(0, NC - 1)], w2_r)
    lane8 = lax.broadcasted_iota(I32, (8, N), 1)

    def regrid(h, total):
        for k in range(CAP):
            rows = pl.ds(pl.multiple_of(h * 32 + k * 8, 8), 8)
            w_x = wbuf[2 * k, h]
            w_yz = wbuf[2 * k + 1, h]
            start = offs[2, 0, h, k]
            here = [lane8 == start + f for f in range(4)]
            value = jnp.zeros((8, N), F32)
            for e in range(4):
                cells = boxes[rows, e * N : (e + 1) * N]
                inner = jnp.zeros((8, N), F32)
                for f in range(4):
                    cell = jnp.sum(jnp.where(here[f], cells, 0.0), axis=1, keepdims=True)
                    inner += cell * w_yz[4 + f : 5 + f, :]
                value += inner * w_yz[e : e + 1, :]
            value = value * w_x
            value = value + pltpu.roll(value, 4, 0)
            value = value + pltpu.roll(value, 2, 0)
            total = total + value * value
            value = value * w_x
            for e in range(4):
                weighted = value * w_yz[e : e + 1, :]
                cells = jnp.zeros((8, N), F32)
                for f in range(4):
                    cell = jnp.sum(weighted * w_yz[4 + f : 5 + f, :], axis=1, keepdims=True)
                    cells = jnp.where(here[f], cell, cells)
                placed[rows, e * N : (e + 1) * N] = cells
        return total

    product_part = lax.fori_loop(0, NT, regrid, jnp.zeros((8, N), F32)) * 0.25

    for e in range(0, 4, 2):
        gacc[...] = jnp.zeros_like(gacc)

        def place(g, carry, e=e):
            rows = pl.ds(pl.multiple_of(g * 256, 256), 256)
            gacc[...] += dot3((pi[0, g], pi[1, g]), split(placed[rows, e * N : (e + 2) * N]))
            return carry

        lax.fori_loop(0, 4, place, 0)
        for i in range(2):
            send2[:, (e + i) * 8 : (e + i + 1) * 8, :] = gacc[:, i * N : (i + 1) * N].reshape(NT, 8, N)

    others(NT, ti, lambda t: push(send2.at[t], recv2.at[rows_of(ti)], (a2_s, a2_r), (ci, t)))
    own_2 = pltpu.make_async_copy(send2.at[ti], recv2.at[rows_of(ti)], loc_sem.at[2])
    own_2.start()

    row8 = lax.broadcasted_iota(I32, (8, N), 0)
    norm_row = jnp.sum(norm_part, axis=0, keepdims=True)
    product_row = jnp.sum(product_part, axis=0, keepdims=True)
    ar1[0] = jnp.where(row8 == 0, norm_row, jnp.where(row8 == 1, product_row, 0.0))
    others(NC, ci, lambda c: push(ar1.at[0], ar1c.at[ci], (r1c_s, r1c_r), (c, ti)))
    ar1c[ci] = ar1[0]
    await_bytes(ar1c.at[pl.ds(0, NC - 1)], r1c_r)
    ar1[1] = jnp.sum(ar1c[...], axis=0)
    others(NT, ti, lambda t: push(ar1.at[1], ar1t.at[ti], (r1t_s, r1t_r), (ci, t)))
    ar1t[ti] = ar1[1]

    own_2.wait()
    await_bytes(recv1.at[pl.ds(0, NT - 1)], a2_r)
    for pair in range(2):
        columns = [
            jnp.concatenate([recv2[pl.ds(c * 4 + 2 * pair + i, N, stride=8), :] for c in range(2)], axis=0)
            for i in range(2)
        ]
        along_y = dot3(right, split(jnp.concatenate(columns, axis=1)))
        parts = [
            jnp.concatenate([along_y[:N, i * N : (i + 1) * N], along_y[N:, i * N : (i + 1) * N]], axis=1)
            for i in range(2)
        ]
        along_z = dot3(split(jnp.concatenate(parts, axis=0)), left)
        for i in range(2):
            xi = 2 * pair + i
            m_re = along_z[i * N : (i + 1) * N, :N]
            m_im = along_z[i * N : (i + 1) * N, N:]
            s_re, s_im = smap[0, xi], smap[1, xi]
            rs_send[:, 0, xi] = (s_re * m_re + s_im * m_im).reshape(NC, 16, N)
            rs_send[:, 1, xi] = (s_re * m_im - s_im * m_re).reshape(NC, 16, N)

    others(NC, ci, lambda c: push(rs_send.at[c], rs_recv.at[ci], (rs_s, rs_r), (c, ti)))
    own_3 = pltpu.make_async_copy(rs_send.at[ci], rs_recv.at[ci], loc_sem.at[3])
    own_3.start()

    loads[4].wait()
    await_bytes(ar1t.at[pl.ds(0, NT - 1)], r1t_r)
    sums = jnp.sum(jnp.sum(ar1t[...], axis=0), axis=1, keepdims=True)
    norm_now, product = sums[0:1], sums[1:2]
    alpha = norm_now / product
    nx[...] = (xv[...].reshape(N, N) + alpha * pbuf[ci].reshape(N, N)).reshape(nx.shape)
    out_x = pltpu.make_async_copy(nx, ox_hbm, out_sem.at[0])
    out_x.start()

    own_3.wait()
    await_bytes(rs_recv.at[pl.ds(0, NC - 1)], rs_r)
    normal = jnp.sum(rs_recv[...], axis=0).reshape(N, N)
    next_r = rv[...].reshape(N, N) - alpha * normal
    nr[...] = next_r.reshape(nr.shape)
    out_r = pltpu.make_async_copy(nr, or_hbm, out_sem.at[1])
    out_r.start()

    ar2[0] = jnp.sum((next_r * next_r).reshape(16, 8, N), axis=0)
    others(NC, ci, lambda c: push(ar2.at[0], ar2c.at[ci], (r2c_s, r2c_r), (c, ti)))
    ar2c[ci] = ar2[0]
    await_bytes(ar2c.at[pl.ds(0, NC - 1)], r2c_r)
    ar2[1] = jnp.sum(ar2c[...], axis=0)
    others(NT, ti, lambda t: push(ar2.at[1], ar2t.at[ti], (r2t_s, r2t_r), (ci, t)))
    ar2t[ti] = ar2[1]
    await_bytes(ar2t.at[pl.ds(0, NT - 1)], r2t_r)
    norm_next = jnp.sum(jnp.sum(jnp.sum(ar2t[...], axis=0), axis=0, keepdims=True), axis=1, keepdims=True)
    beta = norm_next / norm_now
    npv[...] = (nr[...].reshape(N, N) + beta * pbuf[ci].reshape(N, N)).reshape(npv.shape)
    out_p = pltpu.make_async_copy(npv, op_hbm, out_sem.at[2])
    out_p.start()

    await_bytes(pbuf.at[pl.ds(0, NC - 1)], ag_s)
    await_bytes(wbuf.at[0, pl.ds(0, NT - 1)], w1_s)
    await_bytes(wbuf.at[pl.ds(0, NC - 1)], w2_s)
    await_bytes(recv1.at[pl.ds(0, NT - 1)], a1_s)
    await_bytes(recv1.at[pl.ds(0, NT - 1)], a2_s)
    await_bytes(rs_recv.at[pl.ds(0, NC - 1)], rs_s)
    await_bytes(ar1c.at[pl.ds(0, NC - 1)], r1c_s)
    await_bytes(ar1t.at[pl.ds(0, NT - 1)], r1t_s)
    await_bytes(ar2c.at[pl.ds(0, NC - 1)], r2c_s)
    await_bytes(ar2t.at[pl.ds(0, NT - 1)], r2t_s)
    out_x.wait()
    out_r.wait()
    out_p.wait()


def shards(image_p, image_x, image_r, sensitivity, kb_weights, block_owner, owner_list):
    shard = image_p.shape
    vmem = pltpu.VMEM
    dma = pltpu.SemaphoreType.DMA
    scratch = [
        vmem((8, 2 * N, 2 * N), BF16),
        vmem((2, 4, N, N), F32),
        vmem((SLOTS * 12, N), F32),
        vmem(shard, F32),
        vmem(shard, F32),
        vmem((NC,) + shard, F32),
        vmem((NT * 8, N), F32),
        vmem((NC, NT, 8, N), F32),
        vmem((8 * N, 2 * N), BF16),
        vmem((2, 8 * N, 2 * N), BF16),
        vmem((2, 4, 2 * N, 2 * N), BF16),
        vmem((8 * N, N), F32),
        vmem((NT, 32, N), F32),
        vmem((8 * N, 4 * N), F32),
        vmem((8 * N, 4 * N), F32),
        vmem((2 * N, 2 * N), F32),
        vmem((NT, 32, N), F32),
        vmem((8 * N, N), F32),
        vmem((NC,) + shard, F32),
        vmem((NC,) + shard, F32),
        vmem(shard, F32),
        vmem(shard, F32),
        vmem(shard, F32),
        vmem((2, 8, N), F32),
        vmem((NC, 8, N), F32),
        vmem((NT, 8, N), F32),
        vmem((2, 8, N), F32),
        vmem((NC, 8, N), F32),
        vmem((NT, 8, N), F32),
        dma((6,)),
        dma((4,)),
    ]
    scratch += [dma(())] * 20 + [dma((3,))]
    out = jax.ShapeDtypeStruct(shard, F32)
    return pl.pallas_call(
        kernel,
        out_shape=(out, out, out),
        in_specs=[ANY] * 5 + [SMEM] * 2 + [ANY],
        out_specs=(ANY, ANY, ANY),
        scratch_shapes=scratch,
        compiler_params=pltpu.CompilerParams(
            collective_id=0, has_side_effects=True, vmem_limit_bytes=48 * 2**20
        ),
    )(
        image_p, image_x, image_r, sensitivity, kb_weights.reshape(SLOTS * 12, N),
        block_owner, owner_list, jnp.asarray(tables()),
    )


def solution(mesh):
    image = P(None, "tile", "coil", None)
    return jax.shard_map(
        shards,
        mesh=mesh,
        in_specs=(
            image, image, image,
            P("coil", None, "tile", None, None),
            P("tile", None, None, None),
            P("tile"),
            P(None, "tile", None, None),
        ),
        out_specs=(image, image, image),
        check_vma=False,
    )
```

```python
import functools
import math

import jax
import jax.numpy as jnp
import ml_dtypes
import numpy as np
from jax import lax
from jax.experimental import pallas as pl
from jax.experimental.pallas import tpu as pltpu
from jax.sharding import PartitionSpec as P

N = 128
NC = 8
NT = 32
CAP = 4
SLOTS = 32
F32, BF16, I32 = jnp.float32, jnp.bfloat16, jnp.int32
MESH = pl.DeviceIdType.MESH
HBM = pl.BlockSpec(memory_space=pltpu.HBM)
SMEM = pl.BlockSpec(memory_space=pltpu.SMEM)


def tables():
    cells = np.arange(N)
    angle = 2.0 * math.pi / N * ((cells[:, None] * cells[None, :]) % N)
    cos, sin = np.cos(angle) / math.sqrt(N), np.sin(angle) / math.sqrt(N)
    left = np.block([[cos, sin], [-sin, cos]])
    order = [c * N + 4 * t + i for t in range(NT) for c in range(2) for i in range(4)]
    out = []
    for table in (left, left.T, left[:, order], left[:, order].T):
        table = table.astype(np.float32)
        high = table.astype(ml_dtypes.bfloat16)
        low = (table - high.astype(np.float32)).astype(ml_dtypes.bfloat16)
        out += [high, low]
    return np.stack(out)


def split(x):
    high = x.astype(BF16)
    return high, (x - high.astype(F32)).astype(BF16)


def dot(a, b):
    return jnp.dot(a, b, preferred_element_type=F32)


def dot_t(a, b):
    return lax.dot_general(a, b, (((1,), (1,)), ((), ())), preferred_element_type=F32)


def dot3(a, b):
    return dot(a[0], b[0]) + (dot(a[0], b[1]) + dot(a[1], b[0]))


def kernel(
    p_hbm, r_hbm, s_hbm, kb_hbm, own, offs, tab_hbm,
    normal_hbm, alpha_hbm, beta_hbm,
    tab, smap, kb, rv, pbuf, wsend, wbuf, onehot, pt, pi,
    send1, recv1, boxes, placed, send2, recv2, rs_send, rs_near, rs_sum, rs_recv,
    nv, alphas, betas, ar1, ar1c, ar1z, ar1y, ar2, ar2c, ar2z, ar2y,
    load_sem, loc_sem, ag_s, ag_r, agf_s, agf_r, w1_s, w1_r, a1_s, a1_r, a2_s, a2_r, w2f_s, w2f_r, w2_s, w2_r,
    rn_s, rn_r, rs_s, rs_r, r1_s, r1_r, r2_s, r2_r, out_sem,
):
    ci, ti = lax.axis_index("coil"), lax.axis_index("tile")
    core, cx = lax.rem(ci, 2), ci // 2
    near = ci + 1 - 2 * core
    z, y = ti // 4, lax.rem(ti, 4)

    loads = [
        pltpu.make_async_copy(src, dst, load_sem.at[i])
        for i, (src, dst) in enumerate(
            [
                (kb_hbm, kb),
                (tab_hbm, tab),
                (s_hbm.at[0], smap),
                (p_hbm, pbuf.at[ci]),
                (r_hbm, rv),
            ]
        )
    ]

    def partner(me, size, i):
        return lax.rem(me + size // 2 + (i + 1) // 2 * (1 - 2 * lax.rem(i, 2)), size)

    def tiles(body, first=0, last=NT - 1):
        def step(i, carry):
            body(partner(z, 8, lax.rem(i, 8)) * 4 + partner(y, 4, i // 8))
            return carry

        lax.fori_loop(first, last, step, 0)

    def ring(me, size, body):
        def step(i, carry):
            body(partner(me, size, i))
            return carry

        lax.fori_loop(0, size - 1, step, 0)

    barrier = pltpu.get_barrier_semaphore()
    tiles(lambda t: pl.semaphore_signal(barrier, inc=1, device_id=(ci, t), device_id_type=MESH))
    ring(ci, NC, lambda c: pl.semaphore_signal(barrier, inc=1, device_id=(c, ti), device_id_type=MESH))
    for load in loads:
        load.start()

    def push(src, dst, sems, device):
        pltpu.make_async_remote_copy(
            src_ref=src, dst_ref=dst, send_sem=sems[0], recv_sem=sems[1],
            device_id=device, device_id_type=MESH,
        ).start()

    def await_bytes(ref, sem):
        pltpu.make_async_copy(ref, ref, sem).wait()

    class Sum:
        def __init__(self, part, held, slots, sems):
            self.part, self.held, self.slots, self.sems, self.stage = part, held, slots, sems, 0

        def send(self):
            stage = self.stage
            slot, sems = self.slots[stage], (self.sems[0].at[stage], self.sems[1].at[stage])
            self.held[stage] = self.part
            src = self.held.at[stage]
            me = (ci, z, y)[stage]
            device = (lambda i: (i, ti), lambda i: (ci, i * 4 + y), lambda i: (ci, z * 4 + i))[stage]
            ring(me, slot.shape[0], lambda i: push(src, slot.at[me], sems, device(i)))
            slot[me] = self.part

        def take(self):
            slot = self.slots[self.stage]
            await_bytes(slot.at[pl.ds(0, slot.shape[0] - 1)], self.sems[1].at[self.stage])
            self.part = jnp.sum(slot[...], axis=0)
            self.stage += 1
            return self.part

        def sent(self):
            for stage, slot in enumerate(self.slots):
                await_bytes(slot.at[pl.ds(0, slot.shape[0] - 1)], self.sems[0].at[stage])

    sub = lax.broadcasted_iota(I32, (NT, N), 0)
    lane = lax.broadcasted_iota(I32, (NT, N), 1)
    count = jnp.zeros((NT, N), I32)
    pick = jnp.zeros((NT, N), F32)
    for j in range(SLOTS):
        mine = sub == own[j]
        pick = jnp.where(mine & (lane == j) & (count == cx), 1.0, pick)
        count = jnp.where(mine, count + 1, count)
    pick = pick[:, :SLOTS].astype(BF16)
    loads[0].wait()
    for i in range(8):
        row_a = kb[pl.ds(i // 2, SLOTS, stride=12), :]
        row_b = kb[pl.ds(4 + i, SLOTS, stride=12), :]
        row = jnp.where(core == 0, row_a, row_b)
        high = row.astype(BF16)
        mid, low = split(row - high.astype(F32))
        wsend[pl.ds(i, NT, stride=8), :] = dot(pick, high) + (dot(pick, mid) + dot(pick, low))

    pl.semaphore_wait(barrier, NT - 1 + NC - 1)

    def chip(k):
        return lax.rem(ci + 2 * k, NC)

    loads[3].wait()
    mine = pbuf.at[ci]
    for k in (2, 1, 3):
        push(mine, mine, (ag_s.at[k - 1], ag_r.at[k - 1]), (chip(k), ti))
    push(mine, mine, (agf_s, agf_r), (near, ti))

    def send_weights(first, last):
        tiles(lambda t: push(
            wsend.at[pl.ds(pl.multiple_of(t * 8, 8), 8)], wbuf.at[ci, ti], (w1_s, w1_r), (ci, t)), first, last)

    own_w = pltpu.make_async_copy(wsend.at[pl.ds(pl.multiple_of(ti * 8, 8), 8)], wbuf.at[ci, ti], loc_sem.at[0])
    own_w.start()
    send_weights(0, 16)
    for k in (1, 3, 2):
        came = pbuf.at[chip(4 - k)]
        await_bytes(came, ag_r.at[k - 1])
        push(came, came, (agf_s, agf_r), (near, ti))
        if k == 3:
            send_weights(16, 24)
    send_weights(24, NT - 1)

    sub16 = lax.broadcasted_iota(I32, (16, 2 * N), 0)
    lane16 = lax.broadcasted_iota(I32, (16, 2 * N), 1)
    base16 = (sub16 & 1) * N + ((sub16 >> 1) & 3)

    def mark(h, carry):
        for half in range(2):
            start = jnp.where(sub16 < 8, offs[0, 0, 2 * half, h], offs[0, 0, 2 * half + 1, h])
            hit = jnp.where(lane16 == base16 + start, 1.0, 0.0).astype(BF16)
            onehot[pl.ds(pl.multiple_of(h * 32 + half * 16, 16), 16), :] = hit
        return carry

    lax.fori_loop(0, NT, mark, 0)
    loads[1].wait()

    def phases(g, carry):
        rows = pl.ds(pl.multiple_of(g * 256, 256), 256)
        hot = onehot[rows, :]
        for i in range(2):
            pt[i, rows, :] = dot(hot, tab[4 + i]).astype(BF16)
        return carry

    lax.fori_loop(0, 4, phases, 0)
    for i in range(2):
        for g in range(4):
            columns = slice(g * 256, (g + 1) * 256)
            pi[i, :, columns] = dot_t(tab[6 + i], onehot[columns, :]).astype(BF16)

    loads[2].wait()
    await_bytes(pbuf.at[pl.ds(0, 4)], agf_r)
    left, right = (tab[0], tab[1]), (tab[2], tab[3])
    for pair in range(2):
        parts = []
        for xi in (2 * pair, 2 * pair + 1):
            p_re = pbuf[:, 0, xi].reshape(N, N)
            p_im = pbuf[:, 1, xi].reshape(N, N)
            s_re, s_im = smap[0, xi], smap[1, xi]
            parts.append(jnp.concatenate([s_re * p_re - s_im * p_im, s_re * p_im + s_im * p_re], axis=1))
        along_z = dot3(split(jnp.concatenate(parts, axis=0)), right)
        columns = [
            jnp.concatenate([along_z[i * N : (i + 1) * N, :N], along_z[i * N : (i + 1) * N, N:]], axis=0)
            for i in range(2)
        ]
        along_y = dot3(left, split(jnp.concatenate(columns, axis=1)))
        for i in range(2):
            for c in range(2):
                send1[pl.ds(c * 4 + 2 * pair + i, N, stride=8), :] = along_y[
                    c * N : (c + 1) * N, i * N : (i + 1) * N
                ]

    def rows_of(t):
        return pl.ds(pl.multiple_of(t * 32, 32), 32)

    own_w.wait()
    await_bytes(wbuf.at[ci, pl.ds(0, NT - 1)], w1_r)
    for k in (2, 1, 3):
        push(wbuf.at[ci], wbuf.at[ci], (w2_s.at[k - 1], w2_r.at[k - 1]), (chip(k), ti))
    tiles(lambda t: push(send1.at[rows_of(t)], recv1.at[ti], (a1_s, a1_r), (ci, t)))
    own_1 = pltpu.make_async_copy(send1.at[rows_of(ti)], recv1.at[ti], loc_sem.at[1])
    own_1.start()

    push(wbuf.at[ci], wbuf.at[ci], (w2f_s, w2f_r), (near, ti))
    for k in (1, 3, 2):
        came = wbuf.at[chip(4 - k)]
        await_bytes(came, w2_r.at[k - 1])
        push(came, came, (w2f_s, w2f_r), (near, ti))

    loads[4].wait()
    norm_part = jnp.sum(rv[...].reshape(16, 8, N) * rv[...].reshape(16, 8, N), axis=0)

    own_1.wait()
    await_bytes(recv1.at[pl.ds(0, NT - 1)], a1_r)
    for e in range(0, 4, 2):
        got = [recv1[:, (e + i) * 8 : (e + i + 1) * 8, :].reshape(2 * N, N) for i in range(2)]
        field = split(jnp.concatenate(got, axis=1))

        def cut(g, carry, e=e, field=field):
            rows = pl.ds(pl.multiple_of(g * 256, 256), 256)
            boxes[rows, e * N : (e + 2) * N] = dot3((pt[0, rows, :], pt[1, rows, :]), field)
            return carry

        lax.fori_loop(0, 4, cut, 0)

    await_bytes(wbuf.at[pl.ds(0, 4)], w2f_r)
    lane8 = lax.broadcasted_iota(I32, (8, N), 1)
    low8 = lax.broadcasted_iota(I32, (8, N), 0) < 4

    def regrid(g, total):
        spread, pairs, w_xs, starts = [], [], [], []
        for b in range(8):
            h, k = 2 * g + b // 4, b % 4
            w_xs.append(wbuf[2 * k, h])
            w_yz = wbuf[2 * k + 1, h]
            w_z = jnp.where(low8, pltpu.roll(w_yz, 4, 0), w_yz)
            for e in (0, 2):
                pairs.append(jnp.where(low8, w_yz[e : e + 1, :], w_yz[e + 1 : e + 2, :]) * w_z)
            start = offs[2, 0, k, h]
            starts.append(start)
            rows = pl.ds(pl.multiple_of(g * 64 + b * 8, 8), 8)
            moved = jnp.zeros((8, N), F32)
            for e in range(4):
                at = b * 16 + e * 4
                cells = pltpu.roll(boxes[rows, e * N : (e + 1) * N], lax.rem(at + 2 * N - start, N), 1)
                moved = jnp.where((lane8 >= at) & (lane8 < at + 4), cells, moved)
            spread.append(moved)
        pairs = split(jnp.concatenate(pairs, axis=0))
        values = dot3(split(jnp.concatenate(spread, axis=0)), pairs)
        back = []
        for b in range(8):
            value = values[b * 8 : (b + 1) * 8] * w_xs[b]
            value = value + pltpu.roll(value, 4, 0)
            value = value + pltpu.roll(value, 2, 0)
            total = total + value * value
            back.append(value * w_xs[b])
        back = split(jnp.concatenate(back, axis=0))
        cells = dot_t(back[0], pairs[0]) + (dot_t(back[0], pairs[1]) + dot_t(back[1], pairs[0]))
        rows = pl.ds(pl.multiple_of(g * 64, 64), 64)
        for e in range(4):
            parts = []
            for b in range(8):
                at = b * 16 + e * 4
                moved = pltpu.roll(cells[b * 8 : (b + 1) * 8], lax.rem(starts[b] + 2 * N - at, N), 1)
                here = (lane8 >= starts[b]) & (lane8 < starts[b] + 4)
                parts.append(jnp.where(here, moved, 0.0))
            high, low = split(jnp.concatenate(parts, axis=0))
            placed[0, rows, e * N : (e + 1) * N] = high
            placed[1, rows, e * N : (e + 1) * N] = low
        return total

    product_part = lax.fori_loop(0, NT // 2, regrid, jnp.zeros((8, N), F32), unroll=4) * 0.25

    row8 = lax.broadcasted_iota(I32, (8, N), 0)
    norm_row = jnp.sum(norm_part, axis=0, keepdims=True)
    product_row = jnp.sum(product_part, axis=0, keepdims=True)
    both = jnp.where(row8 == 0, norm_row, jnp.where(row8 == 1, product_row, 0.0))
    first_sum = Sum(both, ar1, (ar1c, ar1z, ar1y), (r1_s, r1_r))
    first_sum.send()

    for e in range(0, 4, 2):
        columns = slice(e * N, (e + 2) * N)
        back = dot3((pi[0], pi[1]), (placed[0, :, columns], placed[1, :, columns]))
        for i in range(2):
            send2[:, (e + i) * 8 : (e + i + 1) * 8, :] = back[:, i * N : (i + 1) * N].reshape(NT, 8, N)
    first_sum.take()
    first_sum.send()

    tiles(lambda t: push(send2.at[t], recv2.at[rows_of(ti)], (a2_s, a2_r), (ci, t)))
    own_2 = pltpu.make_async_copy(send2.at[ti], recv2.at[rows_of(ti)], loc_sem.at[2])
    own_2.start()

    first_sum.take()
    first_sum.send()

    own_2.wait()
    await_bytes(recv1.at[pl.ds(0, NT - 1)], a2_r)
    for pair in range(2):
        columns = [
            jnp.concatenate([recv2[pl.ds(c * 4 + 2 * pair + i, N, stride=8), :] for c in range(2)], axis=0)
            for i in range(2)
        ]
        along_y = dot3(right, split(jnp.concatenate(columns, axis=1)))
        parts = [
            jnp.concatenate([along_y[:N, i * N : (i + 1) * N], along_y[N:, i * N : (i + 1) * N]], axis=1)
            for i in range(2)
        ]
        along_z = dot3(split(jnp.concatenate(parts, axis=0)), left)
        for i in range(2):
            m_re = along_z[i * N : (i + 1) * N, :N]
            m_im = along_z[i * N : (i + 1) * N, N:]
            s_re, s_im = smap[0, 2 * pair + i], smap[1, 2 * pair + i]
            for c, back in enumerate((s_re * m_re + s_im * m_im, s_re * m_im - s_im * m_re)):
                back = back.reshape(4, 2, 16, N)
                for half in range(2):
                    rs_send[half, pair, :, c, i] = back[:, half]
        push(rs_send.at[1 - core, pair], rs_near.at[pair], (rn_s.at[pair], rn_r.at[pair]), (near, ti))

    for pair in range(2):
        await_bytes(rs_near.at[pair], rn_r.at[pair])
        rs_sum[pair] = rs_send[core, pair] + rs_near[pair]
        for k in (2, 1, 3):
            to = lax.rem(cx + k, 4)
            push(rs_sum.at[pair, to], rs_recv.at[pair, cx], (rs_s.at[pair], rs_r.at[pair]), (chip(k), ti))
        rs_recv[pair, cx] = rs_sum[pair, cx]
    sums = jnp.sum(first_sum.take(), axis=1, keepdims=True)
    norm_now, product = sums[0:1], sums[1:2]
    alpha = norm_now / product
    norm_next = jnp.zeros((8, N), F32)
    for pair in range(2):
        await_bytes(rs_recv.at[pair, pl.ds(0, 3)], rs_r.at[pair])
        normal = jnp.sum(rs_recv[pair], axis=0)
        nv[:, 2 * pair : 2 * pair + 2] = normal
        next_r = rv[:, 2 * pair : 2 * pair + 2].reshape(64, N) - alpha * normal.reshape(64, N)
        norm_next += jnp.sum((next_r * next_r).reshape(8, 8, N), axis=0)
    out_n = pltpu.make_async_copy(nv, normal_hbm, out_sem.at[0])
    out_n.start()

    alphas[...] = jnp.broadcast_to(alpha, (1, N)).reshape(alphas.shape)
    out_a = pltpu.make_async_copy(alphas, alpha_hbm, out_sem.at[1])
    out_a.start()

    last_sum = Sum(norm_next, ar2, (ar2c, ar2z, ar2y), (r2_s, r2_r))
    for _ in range(3):
        last_sum.send()
        sums = last_sum.take()
    sums = jnp.sum(jnp.sum(sums, axis=0, keepdims=True), axis=1, keepdims=True)
    betas[...] = jnp.broadcast_to(sums / norm_now, (1, N)).reshape(betas.shape)
    out_b = pltpu.make_async_copy(betas, beta_hbm, out_sem.at[2])
    out_b.start()

    for k in range(3):
        await_bytes(pbuf.at[0], ag_s.at[k])
    await_bytes(pbuf.at[pl.ds(0, 4)], agf_s)
    await_bytes(wbuf.at[0, pl.ds(0, NT - 1)], w1_s)
    for k in range(3):
        await_bytes(wbuf.at[0], w2_s.at[k])
    await_bytes(wbuf.at[pl.ds(0, 4)], w2f_s)
    await_bytes(recv1.at[pl.ds(0, NT - 1)], a1_s)
    await_bytes(recv1.at[pl.ds(0, NT - 1)], a2_s)
    for pair in range(2):
        await_bytes(rs_near.at[pair], rn_s.at[pair])
        await_bytes(rs_recv.at[pair, pl.ds(0, 3)], rs_s.at[pair])
    first_sum.sent()
    last_sum.sent()
    out_n.wait()
    out_a.wait()
    out_b.wait()


def shards(image_p, image_x, image_r, sensitivity, kb_weights, block_owner, owner_list):
    shard = image_p.shape
    vmem = pltpu.VMEM
    dma = pltpu.SemaphoreType.DMA
    scratch = [
        vmem((8, 2 * N, 2 * N), BF16),
        vmem((2, 4, N, N), F32),
        vmem((SLOTS * 12, N), F32),
        vmem(shard, F32),
        vmem((NC,) + shard, F32),
        vmem((NT * 8, N), F32),
        vmem((NC, NT, 8, N), F32),
        vmem((8 * N, 2 * N), BF16),
        vmem((2, 8 * N, 2 * N), BF16),
        vmem((2, 2 * N, 8 * N), BF16),
        vmem((8 * N, N), F32),
        vmem((NT, 32, N), F32),
        vmem((8 * N, 4 * N), F32),
        vmem((2, 8 * N, 4 * N), BF16),
        vmem((NT, 32, N), F32),
        vmem((8 * N, N), F32),
        vmem((2, 2, 4, 2, 2, 16, N), F32),
        vmem((2, 4, 2, 2, 16, N), F32),
        vmem((2, 4, 2, 2, 16, N), F32),
        vmem((2, 4, 2, 2, 16, N), F32),
        vmem(shard, F32),
        vmem((1, 1, 1, N), F32),
        vmem((1, 1, 1, N), F32),
    ]
    for _ in range(2):
        scratch += [vmem((3, 8, N), F32)] + [vmem((n, 8, N), F32) for n in (NC, 8, 4)]
    scratch += [dma((n,)) for n in (5, 3, 3, 3)] + [dma(())] * 10
    scratch += [dma((3,))] * 2 + [dma((2,))] * 4 + [dma((3,))] * 5
    step = jax.ShapeDtypeStruct((1, 1, 1, N), F32)
    normal, alpha, beta = pl.pallas_call(
        kernel,
        out_shape=(jax.ShapeDtypeStruct(shard, F32), step, step),
        in_specs=[HBM] * 4 + [SMEM] * 2 + [HBM],
        out_specs=(HBM, HBM, HBM),
        scratch_shapes=scratch,
        compiler_params=pltpu.CompilerParams(
            collective_id=0, has_side_effects=True, vmem_limit_bytes=60 * 2**20
        ),
    )(
        image_p, image_r, sensitivity, kb_weights.reshape(SLOTS * 12, N),
        block_owner, owner_list.transpose(0, 1, 3, 2), jnp.asarray(tables()),
    )
    next_x = image_x + alpha * image_p
    next_r = image_r - alpha * normal
    next_p = next_r + beta * image_p
    return next_x, next_r, next_p


def solution(mesh):
    image = P(None, "tile", "coil", None)
    return jax.shard_map(
        shards,
        mesh=mesh,
        in_specs=(
            image, image, image,
            P("coil", None, "tile", None, None),
            P("tile", None, None, None),
            P("tile"),
            P(None, "tile", None, None),
        ),
        out_specs=(image, image, image),
        check_vma=False,
    )
```

```python
import functools
import math

import jax
import jax.numpy as jnp
import ml_dtypes
import numpy as np
from jax import lax
from jax.experimental import pallas as pl
from jax.experimental.pallas import tpu as pltpu
from jax.sharding import PartitionSpec as P

N = 128
NC = 8
NT = 32
CAP = 4
SLOTS = 32
F32, BF16, I32 = jnp.float32, jnp.bfloat16, jnp.int32
MESH = pl.DeviceIdType.MESH
HBM = pl.BlockSpec(memory_space=pltpu.HBM)
SMEM = pl.BlockSpec(memory_space=pltpu.SMEM)


def tables():
    cells = np.arange(N)
    angle = 2.0 * math.pi / N * ((cells[:, None] * cells[None, :]) % N)
    cos, sin = np.cos(angle) / math.sqrt(N), np.sin(angle) / math.sqrt(N)
    left = np.block([[cos, sin], [-sin, cos]])
    order = [c * N + 4 * t + i for t in range(NT) for c in range(2) for i in range(4)]
    leave = [c * N + 4 * t + 2 * p + i for p in range(2) for t in range(NT) for c in range(2) for i in range(2)]
    out = []
    for table in (left, left.T, left[:, order], left[:, leave].T):
        table = table.astype(np.float32)
        high = table.astype(ml_dtypes.bfloat16)
        low = (table - high.astype(np.float32)).astype(ml_dtypes.bfloat16)
        out += [high, low]
    return np.stack(out)


def split(x):
    high = x.astype(BF16)
    return high, (x - high.astype(F32)).astype(BF16)


def dot(a, b):
    return jnp.dot(a, b, preferred_element_type=F32)


def dot_t(a, b):
    return lax.dot_general(a, b, (((1,), (1,)), ((), ())), preferred_element_type=F32)


def dot3(a, b):
    return dot(a[0], b[0]) + (dot(a[0], b[1]) + dot(a[1], b[0]))


def kernel(
    p_hbm, r_hbm, s_hbm, kb_hbm, own, offs, tab_hbm,
    normal_hbm, alpha_hbm, beta_hbm,
    tab, smap, kb, rv, pbuf, wsend, wbuf, onehot, pt, pi,
    send1, recv1, boxes, placed, send2, recv2, rs_send, rs_near, rs_sum, rs_recv,
    nv, alphas, betas, ar1, ar1c, ar1z, ar1y, ar2, ar2c, ar2z, ar2y,
    load_sem, loc_sem, ag_s, ag_r, agf_s, agf_r, w1_s, w1_r, a1_s, a1_r, w2f_s, w2f_r, w2_s, w2_r, a2_s, a2_r,
    rn_s, rn_r, rs_s, rs_r, r1_s, r1_r, r2_s, r2_r, out_sem,
):
    ci, ti = lax.axis_index("coil"), lax.axis_index("tile")
    core, cx = lax.rem(ci, 2), ci // 2
    near = ci + 1 - 2 * core
    z, y = ti // 4, lax.rem(ti, 4)

    loads = [
        pltpu.make_async_copy(src, dst, load_sem.at[i])
        for i, (src, dst) in enumerate(
            [
                (kb_hbm, kb),
                (tab_hbm, tab),
                (s_hbm.at[0], smap),
                (p_hbm, pbuf.at[ci]),
                (r_hbm, rv),
            ]
        )
    ]

    def partner(me, size, i):
        return lax.rem(me + size // 2 + (i + 1) // 2 * (1 - 2 * lax.rem(i, 2)), size)

    def tiles(body, first=0, last=NT - 1):
        def step(i, carry):
            body(partner(z, 8, lax.rem(i, 8)) * 4 + partner(y, 4, i // 8))
            return carry

        lax.fori_loop(first, last, step, 0)

    def ring(me, size, body):
        def step(i, carry):
            body(partner(me, size, i))
            return carry

        lax.fori_loop(0, size - 1, step, 0)

    barrier = pltpu.get_barrier_semaphore()
    tiles(lambda t: pl.semaphore_signal(barrier, inc=1, device_id=(ci, t), device_id_type=MESH))
    ring(ci, NC, lambda c: pl.semaphore_signal(barrier, inc=1, device_id=(c, ti), device_id_type=MESH))
    for load in loads:
        load.start()

    def push(src, dst, sems, device):
        pltpu.make_async_remote_copy(
            src_ref=src, dst_ref=dst, send_sem=sems[0], recv_sem=sems[1],
            device_id=device, device_id_type=MESH,
        ).start()

    def await_bytes(ref, sem):
        pltpu.make_async_copy(ref, ref, sem).wait()

    class Sum:
        def __init__(self, part, held, slots, sems):
            self.part, self.held, self.slots, self.sems, self.stage = part, held, slots, sems, 0

        def send(self):
            stage = self.stage
            slot, sems = self.slots[stage], (self.sems[0].at[stage], self.sems[1].at[stage])
            self.held[stage] = self.part
            src = self.held.at[stage]
            me = (ci, z, y)[stage]
            device = (lambda i: (i, ti), lambda i: (ci, i * 4 + y), lambda i: (ci, z * 4 + i))[stage]
            ring(me, slot.shape[0], lambda i: push(src, slot.at[me], sems, device(i)))
            slot[me] = self.part

        def take(self):
            slot = self.slots[self.stage]
            await_bytes(slot.at[pl.ds(0, slot.shape[0] - 1)], self.sems[1].at[self.stage])
            self.part = jnp.sum(slot[...], axis=0)
            self.stage += 1
            return self.part

        def sent(self):
            for stage, slot in enumerate(self.slots):
                await_bytes(slot.at[pl.ds(0, slot.shape[0] - 1)], self.sems[0].at[stage])

    sub = lax.broadcasted_iota(I32, (NT, N), 0)
    lane = lax.broadcasted_iota(I32, (NT, N), 1)
    count = jnp.zeros((NT, N), I32)
    pick = jnp.zeros((NT, N), F32)
    for j in range(SLOTS):
        mine = sub == own[j]
        pick = jnp.where(mine & (lane == j) & (count == cx), 1.0, pick)
        count = jnp.where(mine, count + 1, count)
    pick = pick[:, :SLOTS].astype(BF16)
    loads[0].wait()
    for i in range(8):
        row_a = kb[pl.ds(i // 2, SLOTS, stride=12), :]
        row_b = kb[pl.ds(4 + i, SLOTS, stride=12), :]
        row = jnp.where(core == 0, row_a, row_b)
        high = row.astype(BF16)
        mid, low = split(row - high.astype(F32))
        wsend[pl.ds(i, NT, stride=8), :] = dot(pick, high) + (dot(pick, mid) + dot(pick, low))

    pl.semaphore_wait(barrier, NT - 1 + NC - 1)

    def chip(k):
        return lax.rem(ci + 2 * k, NC)

    loads[3].wait()
    mine = pbuf.at[ci]
    for k in (2, 1, 3):
        push(mine, mine, (ag_s.at[k - 1], ag_r.at[k - 1]), (chip(k), ti))
    push(mine, mine, (agf_s, agf_r), (near, ti))

    def send_weights(first, last):
        tiles(lambda t: push(
            wsend.at[pl.ds(pl.multiple_of(t * 8, 8), 8)], wbuf.at[ci, ti], (w1_s, w1_r), (ci, t)), first, last)

    own_w = pltpu.make_async_copy(wsend.at[pl.ds(pl.multiple_of(ti * 8, 8), 8)], wbuf.at[ci, ti], loc_sem.at[0])
    own_w.start()
    send_weights(0, 20)
    for k in (1, 3, 2):
        came = pbuf.at[chip(4 - k)]
        await_bytes(came, ag_r.at[k - 1])
        push(came, came, (agf_s, agf_r), (near, ti))
        if k == 3:
            send_weights(20, 25)
    send_weights(25, NT - 1)

    sub16 = lax.broadcasted_iota(I32, (16, 2 * N), 0)
    lane16 = lax.broadcasted_iota(I32, (16, 2 * N), 1)
    base16 = (sub16 & 1) * N + ((sub16 >> 1) & 3)

    def mark(h, carry):
        for half in range(2):
            start = jnp.where(sub16 < 8, offs[0, 0, 2 * half, h], offs[0, 0, 2 * half + 1, h])
            hit = jnp.where(lane16 == base16 + start, 1.0, 0.0).astype(BF16)
            onehot[pl.ds(pl.multiple_of(h * 32 + half * 16, 16), 16), :] = hit
        return carry

    lax.fori_loop(0, NT, mark, 0)
    loads[1].wait()

    def phases(g, carry):
        rows = pl.ds(pl.multiple_of(g * 256, 256), 256)
        hot = onehot[rows, :]
        for i in range(2):
            pt[i, rows, :] = dot(hot, tab[4 + i]).astype(BF16)
        return carry

    lax.fori_loop(0, 4, phases, 0)
    for i in range(2):
        for g in range(4):
            columns = slice(g * 256, (g + 1) * 256)
            pi[i, :, columns] = dot_t(tab[6 + i], onehot[columns, :]).astype(BF16)

    loads[2].wait()
    await_bytes(pbuf.at[pl.ds(0, 4)], agf_r)
    left, right = (tab[0], tab[1]), (tab[2], tab[3])
    for pair in range(2):
        parts = []
        for xi in (2 * pair, 2 * pair + 1):
            p_re = pbuf[:, 0, xi].reshape(N, N)
            p_im = pbuf[:, 1, xi].reshape(N, N)
            s_re, s_im = smap[0, xi], smap[1, xi]
            parts.append(jnp.concatenate([s_re * p_re - s_im * p_im, s_re * p_im + s_im * p_re], axis=1))
        along_z = dot3(split(jnp.concatenate(parts, axis=0)), right)
        columns = [
            jnp.concatenate([along_z[i * N : (i + 1) * N, :N], along_z[i * N : (i + 1) * N, N:]], axis=0)
            for i in range(2)
        ]
        along_y = dot3(left, split(jnp.concatenate(columns, axis=1)))
        for i in range(2):
            for c in range(2):
                send1[pl.ds(c * 4 + 2 * pair + i, N, stride=8), :] = along_y[
                    c * N : (c + 1) * N, i * N : (i + 1) * N
                ]

    def rows_of(t):
        return pl.ds(pl.multiple_of(t * 32, 32), 32)

    def send_1(t):
        push(send1.at[rows_of(t)], recv1.at[ti], (a1_s, a1_r), (ci, t))

    tiles(send_1, 0, 14)
    own_w.wait()
    await_bytes(wbuf.at[ci, pl.ds(0, NT - 1)], w1_r)
    for k in (2, 1, 3):
        push(wbuf.at[ci], wbuf.at[ci], (w2_s.at[k - 1], w2_r.at[k - 1]), (chip(k), ti))
    tiles(send_1, 14)
    own_1 = pltpu.make_async_copy(send1.at[rows_of(ti)], recv1.at[ti], loc_sem.at[1])
    own_1.start()

    push(wbuf.at[ci], wbuf.at[ci], (w2f_s, w2f_r), (near, ti))
    for k in (1, 3, 2):
        came = wbuf.at[chip(4 - k)]
        await_bytes(came, w2_r.at[k - 1])
        push(came, came, (w2f_s, w2f_r), (near, ti))

    loads[4].wait()
    norm_part = jnp.sum(rv[...].reshape(16, 8, N) * rv[...].reshape(16, 8, N), axis=0)

    own_1.wait()
    await_bytes(recv1.at[pl.ds(0, NT - 1)], a1_r)
    for e in range(0, 4, 2):
        got = [recv1[:, (e + i) * 8 : (e + i + 1) * 8, :].reshape(2 * N, N) for i in range(2)]
        boxes[:, e * N : (e + 2) * N] = dot3((pt[0], pt[1]), split(jnp.concatenate(got, axis=1)))

    await_bytes(wbuf.at[pl.ds(0, 4)], w2f_r)
    lane8 = lax.broadcasted_iota(I32, (8, N), 1)
    low8 = lax.broadcasted_iota(I32, (8, N), 0) < 4

    def regrid(g, total):
        spread, pairs, w_xs, starts = [], [], [], []
        for b in range(8):
            h, k = 2 * g + b // 4, b % 4
            w_xs.append(wbuf[2 * k, h])
            w_yz = wbuf[2 * k + 1, h]
            w_z = jnp.where(low8, pltpu.roll(w_yz, 4, 0), w_yz)
            for e in (0, 2):
                pairs.append(jnp.where(low8, w_yz[e : e + 1, :], w_yz[e + 1 : e + 2, :]) * w_z)
            start = offs[2, 0, k, h]
            starts.append(start)
            rows = pl.ds(pl.multiple_of(g * 64 + b * 8, 8), 8)
            moved = jnp.zeros((8, N), F32)
            for e in range(4):
                at = b * 16 + e * 4
                cells = pltpu.roll(boxes[rows, e * N : (e + 1) * N], lax.rem(at + 2 * N - start, N), 1)
                moved = jnp.where((lane8 >= at) & (lane8 < at + 4), cells, moved)
            spread.append(moved)
        pairs = split(jnp.concatenate(pairs, axis=0))
        values = dot3(split(jnp.concatenate(spread, axis=0)), pairs)
        back = []
        for b in range(8):
            value = values[b * 8 : (b + 1) * 8] * w_xs[b]
            value = value + pltpu.roll(value, 4, 0)
            value = value + pltpu.roll(value, 2, 0)
            total = total + value * value
            back.append(value * w_xs[b])
        back = split(jnp.concatenate(back, axis=0))
        cells = dot_t(back[0], pairs[0]) + (dot_t(back[0], pairs[1]) + dot_t(back[1], pairs[0]))
        rows = pl.ds(pl.multiple_of(g * 64, 64), 64)
        for e in range(4):
            parts = []
            for b in range(8):
                at = b * 16 + e * 4
                moved = pltpu.roll(cells[b * 8 : (b + 1) * 8], lax.rem(starts[b] + 2 * N - at, N), 1)
                here = (lane8 >= starts[b]) & (lane8 < starts[b] + 4)
                parts.append(jnp.where(here, moved, 0.0))
            high, low = split(jnp.concatenate(parts, axis=0))
            placed[0, rows, e * N : (e + 1) * N] = high
            placed[1, rows, e * N : (e + 1) * N] = low
        return total

    product_part = lax.fori_loop(0, NT // 2, regrid, jnp.zeros((8, N), F32), unroll=4) * 0.25

    row8 = lax.broadcasted_iota(I32, (8, N), 0)
    norm_row = jnp.sum(norm_part, axis=0, keepdims=True)
    product_row = jnp.sum(product_part, axis=0, keepdims=True)
    both = jnp.where(row8 == 0, norm_row, jnp.where(row8 == 1, product_row, 0.0))
    first_sum = Sum(both, ar1, (ar1c, ar1z, ar1y), (r1_s, r1_r))
    first_sum.send()

    low = lax.rem(lax.broadcasted_iota(I32, (2 * N, N), 0), 8) < 4
    for e in range(2):
        columns = slice(2 * e * N, (2 * e + 2) * N)
        back = dot3((pi[0], pi[1]), (placed[0, :, columns], placed[1, :, columns]))
        one, two = back[:, :N], back[:, N:]
        even = jnp.where(low, one, pltpu.roll(two, 4, 0))
        odd = jnp.where(low, pltpu.roll(one, 2 * N - 4, 0), two)
        send2[:, :, 0, e * 8 : (e + 1) * 8, :] = even.reshape(2, NT // 2, 8, N)
        send2[:, :, 1, e * 8 : (e + 1) * 8, :] = odd.reshape(2, NT // 2, 8, N)

    def place_of(t):
        return pl.ds(pl.multiple_of(t * 16, 16), 16)

    owns = []
    for pair in range(2):
        tiles(lambda t, pair=pair: push(
            send2.at[pair, t // 2, lax.rem(t, 2)], recv2.at[pair, place_of(ti)],
            (a2_s.at[pair], a2_r.at[pair]), (ci, t)))
        owns.append(pltpu.make_async_copy(
            send2.at[pair, ti // 2, lax.rem(ti, 2)], recv2.at[pair, place_of(ti)], loc_sem.at[2 + pair]))
        owns[pair].start()
    first_sum.take()
    first_sum.send()

    def spread_sum(pair):
        await_bytes(rs_near.at[pair], rn_r.at[pair])
        rs_sum[pair] = rs_send[core, pair] + rs_near[pair]
        for k in (2, 1, 3):
            to = lax.rem(cx + k, 4)
            push(rs_sum.at[pair, to], rs_recv.at[pair, cx], (rs_s.at[pair], rs_r.at[pair]), (chip(k), ti))
        rs_recv[pair, cx] = rs_sum[pair, cx]

    for pair in range(2):
        owns[pair].wait()
        await_bytes(recv2.at[pair, pl.ds(0, 16 * (NT - 1))], a2_r.at[pair])
        columns = [
            jnp.concatenate([recv2[pair, pl.ds(c * 2 + i, N, stride=4), :] for c in range(2)], axis=0)
            for i in range(2)
        ]
        along_y = dot3(right, split(jnp.concatenate(columns, axis=1)))
        parts = [
            jnp.concatenate([along_y[:N, i * N : (i + 1) * N], along_y[N:, i * N : (i + 1) * N]], axis=1)
            for i in range(2)
        ]
        along_z = dot3(split(jnp.concatenate(parts, axis=0)), left)
        for i in range(2):
            m_re = along_z[i * N : (i + 1) * N, :N]
            m_im = along_z[i * N : (i + 1) * N, N:]
            s_re, s_im = smap[0, 2 * pair + i], smap[1, 2 * pair + i]
            for c, back in enumerate((s_re * m_re + s_im * m_im, s_re * m_im - s_im * m_re)):
                back = back.reshape(4, 2, 16, N)
                for half in range(2):
                    rs_send[half, pair, :, c, i] = back[:, half]
        push(rs_send.at[1 - core, pair], rs_near.at[pair], (rn_s.at[pair], rn_r.at[pair]), (near, ti))
        if pair == 0:
            spread_sum(0)
            first_sum.take()
            first_sum.send()
    spread_sum(1)
    sums = jnp.sum(first_sum.take(), axis=1, keepdims=True)
    norm_now, product = sums[0:1], sums[1:2]
    alpha = norm_now / product
    norm_next = jnp.zeros((8, N), F32)
    for pair in range(2):
        await_bytes(rs_recv.at[pair, pl.ds(0, 3)], rs_r.at[pair])
        normal = jnp.sum(rs_recv[pair], axis=0)
        nv[:, 2 * pair : 2 * pair + 2] = normal
        next_r = rv[:, 2 * pair : 2 * pair + 2].reshape(64, N) - alpha * normal.reshape(64, N)
        norm_next += jnp.sum((next_r * next_r).reshape(8, 8, N), axis=0)
    out_n = pltpu.make_async_copy(nv, normal_hbm, out_sem.at[0])
    out_n.start()

    alphas[...] = jnp.broadcast_to(alpha, (1, N)).reshape(alphas.shape)
    out_a = pltpu.make_async_copy(alphas, alpha_hbm, out_sem.at[1])
    out_a.start()

    last_sum = Sum(norm_next, ar2, (ar2c, ar2z, ar2y), (r2_s, r2_r))
    for _ in range(3):
        last_sum.send()
        sums = last_sum.take()
    sums = jnp.sum(jnp.sum(sums, axis=0, keepdims=True), axis=1, keepdims=True)
    betas[...] = jnp.broadcast_to(sums / norm_now, (1, N)).reshape(betas.shape)
    out_b = pltpu.make_async_copy(betas, beta_hbm, out_sem.at[2])
    out_b.start()

    for k in range(3):
        await_bytes(pbuf.at[0], ag_s.at[k])
    await_bytes(pbuf.at[pl.ds(0, 4)], agf_s)
    await_bytes(wbuf.at[0, pl.ds(0, NT - 1)], w1_s)
    for k in range(3):
        await_bytes(wbuf.at[0], w2_s.at[k])
    await_bytes(wbuf.at[pl.ds(0, 4)], w2f_s)
    await_bytes(recv1.at[pl.ds(0, NT - 1)], a1_s)
    for pair in range(2):
        await_bytes(recv2.at[pair, pl.ds(0, 16 * (NT - 1))], a2_s.at[pair])
        await_bytes(rs_near.at[pair], rn_s.at[pair])
        await_bytes(rs_recv.at[pair, pl.ds(0, 3)], rs_s.at[pair])
    first_sum.sent()
    last_sum.sent()
    out_n.wait()
    out_a.wait()
    out_b.wait()


def shards(image_p, image_x, image_r, sensitivity, kb_weights, block_owner, owner_list):
    shard = image_p.shape
    vmem = pltpu.VMEM
    dma = pltpu.SemaphoreType.DMA
    scratch = [
        vmem((8, 2 * N, 2 * N), BF16),
        vmem((2, 4, N, N), F32),
        vmem((SLOTS * 12, N), F32),
        vmem(shard, F32),
        vmem((NC,) + shard, F32),
        vmem((NT * 8, N), F32),
        vmem((NC, NT, 8, N), F32),
        vmem((8 * N, 2 * N), BF16),
        vmem((2, 8 * N, 2 * N), BF16),
        vmem((2, 2 * N, 8 * N), BF16),
        vmem((8 * N, N), F32),
        vmem((NT, 32, N), F32),
        vmem((8 * N, 4 * N), F32),
        vmem((2, 8 * N, 4 * N), BF16),
        vmem((2, NT // 2, 2, 16, N), F32),
        vmem((2, 4 * N, N), F32),
        vmem((2, 2, 4, 2, 2, 16, N), F32),
        vmem((2, 4, 2, 2, 16, N), F32),
        vmem((2, 4, 2, 2, 16, N), F32),
        vmem((2, 4, 2, 2, 16, N), F32),
        vmem(shard, F32),
        vmem((1, 1, 1, N), F32),
        vmem((1, 1, 1, N), F32),
    ]
    for _ in range(2):
        scratch += [vmem((3, 8, N), F32)] + [vmem((n, 8, N), F32) for n in (NC, 8, 4)]
    scratch += [dma((n,)) for n in (5, 4, 3, 3)] + [dma(())] * 8
    scratch += [dma((3,))] * 2 + [dma((2,))] * 6 + [dma((3,))] * 5
    step = jax.ShapeDtypeStruct((1, 1, 1, N), F32)
    normal, alpha, beta = pl.pallas_call(
        kernel,
        out_shape=(jax.ShapeDtypeStruct(shard, F32), step, step),
        in_specs=[HBM] * 4 + [SMEM] * 2 + [HBM],
        out_specs=(HBM, HBM, HBM),
        scratch_shapes=scratch,
        compiler_params=pltpu.CompilerParams(
            collective_id=0, has_side_effects=True, vmem_limit_bytes=60 * 2**20
        ),
    )(
        image_p, image_r, sensitivity, kb_weights.reshape(SLOTS * 12, N),
        block_owner, owner_list.transpose(0, 1, 3, 2), jnp.asarray(tables()),
    )
    next_x = image_x + alpha * image_p
    next_r = image_r - alpha * normal
    next_p = next_r + beta * image_p
    return next_x, next_r, next_p


def solution(mesh):
    image = P(None, "tile", "coil", None)
    return jax.shard_map(
        shards,
        mesh=mesh,
        in_specs=(
            image, image, image,
            P("coil", None, "tile", None, None),
            P("tile", None, None, None),
            P("tile"),
            P(None, "tile", None, None),
        ),
        out_specs=(image, image, image),
        check_vma=False,
    )
```

```python
import functools
import math

import jax
import jax.numpy as jnp
import ml_dtypes
import numpy as np
from jax import lax
from jax.experimental import pallas as pl
from jax.experimental.pallas import tpu as pltpu
from jax.sharding import PartitionSpec as P

N = 128
NC = 8
NT = 32
CAP = 4
SLOTS = 32
F32, BF16, I32 = jnp.float32, jnp.bfloat16, jnp.int32
MESH = pl.DeviceIdType.MESH
HBM = pl.BlockSpec(memory_space=pltpu.HBM)
SMEM = pl.BlockSpec(memory_space=pltpu.SMEM)


def tables():
    cells = np.arange(N)
    angle = 2.0 * math.pi / N * ((cells[:, None] * cells[None, :]) % N)
    cos, sin = np.cos(angle) / math.sqrt(N), np.sin(angle) / math.sqrt(N)
    left = np.block([[cos, sin], [-sin, cos]])
    order = [c * N + 4 * t + i for t in range(NT) for c in range(2) for i in range(4)]
    leave = [c * N + 4 * t + 2 * p + i for p in range(2) for t in range(NT) for c in range(2) for i in range(2)]
    out = []
    for table in (left, left.T, left[:, order], left[:, leave].T):
        table = table.astype(np.float32)
        high = table.astype(ml_dtypes.bfloat16)
        low = (table - high.astype(np.float32)).astype(ml_dtypes.bfloat16)
        out += [high, low]
    return np.stack(out)


def split(x):
    high = x.astype(BF16)
    return high, (x - high.astype(F32)).astype(BF16)


def dot(a, b):
    return jnp.dot(a, b, preferred_element_type=F32)


def dot_t(a, b):
    return lax.dot_general(a, b, (((1,), (1,)), ((), ())), preferred_element_type=F32)


def dot3(a, b):
    return dot(a[0], b[0]) + (dot(a[0], b[1]) + dot(a[1], b[0]))


def kernel(
    p_hbm, r_hbm, s_hbm, kb_hbm, own, offs, tab_hbm,
    normal_hbm, alpha_hbm, beta_hbm,
    tab, smap, kb, rv, pbuf, wsend, wbuf, onehot, pt, pi,
    send1, recv1, boxes, placed, send2, recv2, rs_send, rs_near, rs_sum, rs_recv,
    nv, alphas, betas, ar1, ar1c, ar1z, ar1y, ar2, ar2a, ar2b,
    load_sem, loc_sem, ag_s, ag_r, agf_s, agf_r, w1_s, w1_r, a1_s, a1_r, w2f_s, w2f_r, w2_s, w2_r, a2_s, a2_r,
    rn_s, rn_r, rs_s, rs_r, r1_s, r1_r, r2_s, r2_r, out_sem,
):
    ci, ti = lax.axis_index("coil"), lax.axis_index("tile")
    core, cx = lax.rem(ci, 2), ci // 2
    near = ci + 1 - 2 * core
    z, y = ti // 4, lax.rem(ti, 4)

    loads = [
        pltpu.make_async_copy(src, dst, load_sem.at[i])
        for i, (src, dst) in enumerate(
            [
                (kb_hbm, kb),
                (tab_hbm, tab),
                (s_hbm.at[0], smap),
                (p_hbm, pbuf.at[ci]),
                (r_hbm, rv),
            ]
        )
    ]

    def partner(me, size, i):
        return lax.rem(me + size // 2 + (i + 1) // 2 * (1 - 2 * lax.rem(i, 2)), size)

    def tiles(body, first=0, last=NT - 1):
        def step(i, carry):
            body(partner(z, 8, lax.rem(i, 8)) * 4 + partner(y, 4, i // 8))
            return carry

        lax.fori_loop(first, last, step, 0)

    def ring(me, size, body):
        def step(i, carry):
            body(partner(me, size, i))
            return carry

        lax.fori_loop(0, size - 1, step, 0)

    barrier = pltpu.get_barrier_semaphore()
    tiles(lambda t: pl.semaphore_signal(barrier, inc=1, device_id=(ci, t), device_id_type=MESH))
    ring(ci, NC, lambda c: pl.semaphore_signal(barrier, inc=1, device_id=(c, ti), device_id_type=MESH))

    def greet(count, device):
        def step(i, carry):
            pl.semaphore_signal(barrier, inc=1, device_id=device(i), device_id_type=MESH)
            return carry

        lax.fori_loop(0, count, step, 0)

    for load in loads:
        load.start()

    def push(src, dst, sems, device):
        pltpu.make_async_remote_copy(
            src_ref=src, dst_ref=dst, send_sem=sems[0], recv_sem=sems[1],
            device_id=device, device_id_type=MESH,
        ).start()

    def await_bytes(ref, sem):
        pltpu.make_async_copy(ref, ref, sem).wait()

    over_coil = (NC, ci, lambda i: (partner(ci, NC, i), ti))
    over_z = (8, z, lambda i: (ci, partner(z, 8, i) * 4 + y))
    over_y = (4, y, lambda i: (ci, z * 4 + partner(y, 4, i)))
    over_tile = (32, ti, lambda i: (ci, partner(z, 8, lax.rem(i, 8)) * 4 + partner(y, 4, i // 8)))

    class Sum:
        def __init__(self, part, stages, held, slots, sems):
            self.part, self.stages, self.held, self.slots, self.sems, self.stage = part, stages, held, slots, sems, 0

        def send(self):
            stage = self.stage
            slot, sems = self.slots[stage], (self.sems[0].at[stage], self.sems[1].at[stage])
            self.held[stage] = self.part
            src = self.held.at[stage]
            size, me, device = self.stages[stage]

            def step(i, carry):
                push(src, slot.at[me], sems, device(i))
                return carry

            lax.fori_loop(0, size - 1, step, 0)
            slot[me] = self.part

        def take(self):
            slot = self.slots[self.stage]
            await_bytes(slot.at[pl.ds(0, slot.shape[0] - 1)], self.sems[1].at[self.stage])
            self.part = jnp.sum(slot[...], axis=0)
            self.stage += 1
            return self.part

        def sent(self):
            for stage, slot in enumerate(self.slots):
                await_bytes(slot.at[pl.ds(0, slot.shape[0] - 1)], self.sems[0].at[stage])

    sub = lax.broadcasted_iota(I32, (NT, N), 0)
    lane = lax.broadcasted_iota(I32, (NT, N), 1)
    count = jnp.zeros((NT, N), I32)
    pick = jnp.zeros((NT, N), F32)
    for j in range(SLOTS):
        mine = sub == own[j]
        pick = jnp.where(mine & (lane == j) & (count == cx), 1.0, pick)
        count = jnp.where(mine, count + 1, count)
    pick = pick[:, :SLOTS].astype(BF16)
    loads[0].wait()
    for i in range(8):
        row_a = kb[pl.ds(i // 2, SLOTS, stride=12), :]
        row_b = kb[pl.ds(4 + i, SLOTS, stride=12), :]
        row = jnp.where(core == 0, row_a, row_b)
        high = row.astype(BF16)
        mid, low = split(row - high.astype(F32))
        wsend[pl.ds(i, NT, stride=8), :] = dot(pick, high) + (dot(pick, mid) + dot(pick, low))

    pl.semaphore_wait(barrier, NT - 1 + NC - 1)

    def chip(k):
        return lax.rem(ci + 2 * k, NC)

    loads[3].wait()
    mine = pbuf.at[ci]
    for k in (2, 1, 3):
        push(mine, mine, (ag_s.at[k - 1], ag_r.at[k - 1]), (chip(k), ti))
    push(mine, mine, (agf_s, agf_r), (near, ti))

    def send_weights(first, last):
        tiles(lambda t: push(
            wsend.at[pl.ds(pl.multiple_of(t * 8, 8), 8)], wbuf.at[ci, ti], (w1_s, w1_r), (ci, t)), first, last)

    own_w = pltpu.make_async_copy(wsend.at[pl.ds(pl.multiple_of(ti * 8, 8), 8)], wbuf.at[ci, ti], loc_sem.at[0])
    own_w.start()
    send_weights(0, 14)
    for k in (1, 3, 2):
        came = pbuf.at[chip(4 - k)]
        await_bytes(came, ag_r.at[k - 1])
        push(came, came, (agf_s, agf_r), (near, ti))
        if k == 3:
            send_weights(14, 21)
    send_weights(21, NT - 1)

    sub16 = lax.broadcasted_iota(I32, (16, 2 * N), 0)
    lane16 = lax.broadcasted_iota(I32, (16, 2 * N), 1)
    base16 = (sub16 & 1) * N + ((sub16 >> 1) & 3)

    def mark(h, carry):
        for half in range(2):
            start = jnp.where(sub16 < 8, offs[0, 0, 2 * half, h], offs[0, 0, 2 * half + 1, h])
            hit = jnp.where(lane16 == base16 + start, 1.0, 0.0).astype(BF16)
            onehot[pl.ds(pl.multiple_of(h * 32 + half * 16, 16), 16), :] = hit
        return carry

    lax.fori_loop(0, NT, mark, 0)
    loads[1].wait()

    def phases(g, carry):
        rows = pl.ds(pl.multiple_of(g * 256, 256), 256)
        hot = onehot[rows, :]
        for i in range(2):
            pt[i, rows, :] = dot(hot, tab[4 + i]).astype(BF16)
        return carry

    lax.fori_loop(0, 4, phases, 0)
    for i in range(2):
        for g in range(4):
            columns = slice(g * 256, (g + 1) * 256)
            pi[i * 2 * N : (i + 1) * 2 * N, columns] = dot_t(tab[6 + i], onehot[columns, :]).astype(BF16)

    loads[2].wait()
    await_bytes(pbuf.at[pl.ds(0, 4)], agf_r)
    left, right = (tab[0], tab[1]), (tab[2], tab[3])
    for pair in range(2):
        parts = []
        for xi in (2 * pair, 2 * pair + 1):
            p_re = pbuf[:, 0, xi].reshape(N, N)
            p_im = pbuf[:, 1, xi].reshape(N, N)
            s_re, s_im = smap[0, xi], smap[1, xi]
            parts.append(jnp.concatenate([s_re * p_re - s_im * p_im, s_re * p_im + s_im * p_re], axis=1))
        along_z = dot3(split(jnp.concatenate(parts, axis=0)), right)
        columns = [
            jnp.concatenate([along_z[i * N : (i + 1) * N, :N], along_z[i * N : (i + 1) * N, N:]], axis=0)
            for i in range(2)
        ]
        along_y = dot3(left, split(jnp.concatenate(columns, axis=1)))
        for i in range(2):
            for c in range(2):
                send1[pl.ds(c * 4 + 2 * pair + i, N, stride=8), :] = along_y[
                    c * N : (c + 1) * N, i * N : (i + 1) * N
                ]

    def rows_of(t):
        return pl.ds(pl.multiple_of(t * 32, 32), 32)

    def send_1(t):
        push(send1.at[rows_of(t)], recv1.at[ti], (a1_s, a1_r), (ci, t))

    tiles(send_1, 0, 14)
    own_w.wait()
    await_bytes(wbuf.at[ci, pl.ds(0, NT - 1)], w1_r)
    for k in (2, 1, 3):
        push(wbuf.at[ci], wbuf.at[ci], (w2_s.at[k - 1], w2_r.at[k - 1]), (chip(k), ti))
    tiles(send_1, 14)
    own_1 = pltpu.make_async_copy(send1.at[rows_of(ti)], recv1.at[ti], loc_sem.at[1])
    own_1.start()

    push(wbuf.at[ci], wbuf.at[ci], (w2f_s, w2f_r), (near, ti))
    for k in (1, 3, 2):
        came = wbuf.at[chip(4 - k)]
        await_bytes(came, w2_r.at[k - 1])
        push(came, came, (w2f_s, w2f_r), (near, ti))

    loads[4].wait()
    norm_part = jnp.sum(rv[...].reshape(16, 8, N) * rv[...].reshape(16, 8, N), axis=0)

    own_1.wait()
    await_bytes(recv1.at[pl.ds(0, NT - 1)], a1_r)
    for e in range(0, 4, 2):
        got = [recv1[:, (e + i) * 8 : (e + i + 1) * 8, :].reshape(2 * N, N) for i in range(2)]
        boxes[:, e * N : (e + 2) * N] = dot3((pt[0], pt[1]), split(jnp.concatenate(got, axis=1)))

    await_bytes(wbuf.at[pl.ds(0, 4)], w2f_r)
    lane8 = lax.broadcasted_iota(I32, (8, N), 1)
    low8 = lax.broadcasted_iota(I32, (8, N), 0) < 4

    def regrid(g, total):
        spread, pairs, w_xs, starts = [], [], [], []
        for b in range(8):
            h, k = 2 * g + b // 4, b % 4
            w_xs.append(wbuf[2 * k, h])
            w_yz = wbuf[2 * k + 1, h]
            w_z = jnp.where(low8, pltpu.roll(w_yz, 4, 0), w_yz)
            for e in (0, 2):
                pairs.append(jnp.where(low8, w_yz[e : e + 1, :], w_yz[e + 1 : e + 2, :]) * w_z)
            start = offs[2, 0, k, h]
            starts.append(start)
            rows = pl.ds(pl.multiple_of(g * 64 + b * 8, 8), 8)
            moved = jnp.zeros((8, N), F32)
            for e in range(4):
                at = b * 16 + e * 4
                cells = pltpu.roll(boxes[rows, e * N : (e + 1) * N], lax.rem(at + 2 * N - start, N), 1)
                moved = jnp.where((lane8 >= at) & (lane8 < at + 4), cells, moved)
            spread.append(moved)
        pairs = split(jnp.concatenate(pairs, axis=0))
        values = dot3(split(jnp.concatenate(spread, axis=0)), pairs)
        back = []
        for b in range(8):
            value = values[b * 8 : (b + 1) * 8] * w_xs[b]
            value = value + pltpu.roll(value, 4, 0)
            value = value + pltpu.roll(value, 2, 0)
            total = total + value * value
            back.append(value * w_xs[b])
        back = split(jnp.concatenate(back, axis=0))
        cells = dot_t(back[0], pairs[0]) + (dot_t(back[0], pairs[1]) + dot_t(back[1], pairs[0]))
        rows = pl.ds(pl.multiple_of(g * 64, 64), 64)
        for e in range(4):
            parts = []
            for b in range(8):
                at = b * 16 + e * 4
                moved = pltpu.roll(cells[b * 8 : (b + 1) * 8], lax.rem(starts[b] + 2 * N - at, N), 1)
                here = (lane8 >= starts[b]) & (lane8 < starts[b] + 4)
                parts.append(jnp.where(here, moved, 0.0))
            high, low = split(jnp.concatenate(parts, axis=0))
            placed[0, rows, e * N : (e + 1) * N] = high
            placed[1, rows, e * N : (e + 1) * N] = low
        return total

    product_part = lax.fori_loop(0, NT // 2, regrid, jnp.zeros((8, N), F32), unroll=16) * 0.25

    row8 = lax.broadcasted_iota(I32, (8, N), 0)
    norm_row = jnp.sum(norm_part, axis=0, keepdims=True)
    product_row = jnp.sum(product_part, axis=0, keepdims=True)
    both = jnp.where(row8 == 0, norm_row, jnp.where(row8 == 1, product_row, 0.0))
    first_sum = Sum(both, (over_coil, over_z, over_y), ar1, (ar1c, ar1z, ar1y), (r1_s, r1_r))

    low = lax.rem(lax.broadcasted_iota(I32, (2 * N, N), 0), 8) < 4
    for e in range(2):
        columns = slice(2 * e * N, (2 * e + 2) * N)
        both_terms = dot(pi[...], placed[0, :, columns])
        back = both_terms[: 2 * N] + (both_terms[2 * N :] + dot(pi[: 2 * N], placed[1, :, columns]))
        one, two = back[:, :N], back[:, N:]
        even = jnp.where(low, one, pltpu.roll(two, 4, 0))
        odd = jnp.where(low, pltpu.roll(one, 2 * N - 4, 0), two)
        send2[:, :, 0, e * 8 : (e + 1) * 8, :] = even.reshape(2, NT // 2, 8, N)
        send2[:, :, 1, e * 8 : (e + 1) * 8, :] = odd.reshape(2, NT // 2, 8, N)

    def place_of(t):
        return pl.ds(pl.multiple_of(t * 16, 16), 16)

    owns = []
    for pair in range(2):
        tiles(lambda t, pair=pair: push(
            send2.at[pair, t // 2, lax.rem(t, 2)], recv2.at[pair, place_of(ti)],
            (a2_s.at[pair], a2_r.at[pair]), (ci, t)))
        owns.append(pltpu.make_async_copy(
            send2.at[pair, ti // 2, lax.rem(ti, 2)], recv2.at[pair, place_of(ti)], loc_sem.at[2 + pair]))
        owns[pair].start()
        if pair == 0:
            first_sum.send()
    first_sum.take()
    first_sum.send()

    def spread_sum(pair):
        await_bytes(rs_near.at[pair], rn_r.at[pair])
        rs_sum[pair] = rs_send[core, pair] + rs_near[pair]
        for k in (2, 1, 3):
            to = lax.rem(cx + k, 4)
            push(rs_sum.at[pair, to], rs_recv.at[pair, cx], (rs_s.at[pair], rs_r.at[pair]), (chip(k), ti))
        rs_recv[pair, cx] = rs_sum[pair, cx]

    for pair in range(2):
        owns[pair].wait()
        await_bytes(recv2.at[pair, pl.ds(0, 16 * (NT - 1))], a2_r.at[pair])
        columns = [
            jnp.concatenate([recv2[pair, pl.ds(c * 2 + i, N, stride=4), :] for c in range(2)], axis=0)
            for i in range(2)
        ]
        along_y = dot3(right, split(jnp.concatenate(columns, axis=1)))
        parts = [
            jnp.concatenate([along_y[:N, i * N : (i + 1) * N], along_y[N:, i * N : (i + 1) * N]], axis=1)
            for i in range(2)
        ]
        along_z = dot3(split(jnp.concatenate(parts, axis=0)), left)
        for i in range(2):
            m_re = along_z[i * N : (i + 1) * N, :N]
            m_im = along_z[i * N : (i + 1) * N, N:]
            s_re, s_im = smap[0, 2 * pair + i], smap[1, 2 * pair + i]
            for c, back in enumerate((s_re * m_re + s_im * m_im, s_re * m_im - s_im * m_re)):
                back = back.reshape(4, 2, 16, N)
                for half in range(2):
                    rs_send[half, pair, :, c, i] = back[:, half]
        push(rs_send.at[1 - core, pair], rs_near.at[pair], (rn_s.at[pair], rn_r.at[pair]), (near, ti))
        if pair == 0:
            spread_sum(0)
            first_sum.take()
            first_sum.send()
    spread_sum(1)
    sums = jnp.sum(first_sum.take(), axis=1, keepdims=True)
    norm_now, product = sums[0:1], sums[1:2]
    alpha = norm_now / product
    norm_next = jnp.zeros((8, N), F32)
    for pair in range(2):
        await_bytes(rs_recv.at[pair, pl.ds(0, 3)], rs_r.at[pair])
        normal = jnp.sum(rs_recv[pair], axis=0)
        nv[:, 2 * pair : 2 * pair + 2] = normal
        next_r = rv[:, 2 * pair : 2 * pair + 2].reshape(64, N) - alpha * normal.reshape(64, N)
        norm_next += jnp.sum((next_r * next_r).reshape(8, 8, N), axis=0)
    out_n = pltpu.make_async_copy(nv, normal_hbm, out_sem.at[0])
    out_n.start()

    alphas[...] = jnp.broadcast_to(alpha, (1, N)).reshape(alphas.shape)
    out_a = pltpu.make_async_copy(alphas, alpha_hbm, out_sem.at[1])
    out_a.start()

    last_sum = Sum(norm_next, (over_coil, over_tile), ar2, (ar2a, ar2b), (r2_s, r2_r))
    for _ in range(2):
        last_sum.send()
        sums = last_sum.take()
    sums = jnp.sum(jnp.sum(sums, axis=0, keepdims=True), axis=1, keepdims=True)
    betas[...] = jnp.broadcast_to(sums / norm_now, (1, N)).reshape(betas.shape)
    out_b = pltpu.make_async_copy(betas, beta_hbm, out_sem.at[2])
    out_b.start()

    for k in range(3):
        await_bytes(pbuf.at[0], ag_s.at[k])
    await_bytes(pbuf.at[pl.ds(0, 4)], agf_s)
    await_bytes(wbuf.at[0, pl.ds(0, NT - 1)], w1_s)
    for k in range(3):
        await_bytes(wbuf.at[0], w2_s.at[k])
    await_bytes(wbuf.at[pl.ds(0, 4)], w2f_s)
    await_bytes(recv1.at[pl.ds(0, NT - 1)], a1_s)
    for pair in range(2):
        await_bytes(recv2.at[pair, pl.ds(0, 16 * (NT - 1))], a2_s.at[pair])
        await_bytes(rs_near.at[pair], rn_s.at[pair])
        await_bytes(rs_recv.at[pair, pl.ds(0, 3)], rs_s.at[pair])
    first_sum.sent()
    last_sum.sent()
    out_n.wait()
    out_a.wait()
    out_b.wait()


def shards(image_p, image_x, image_r, sensitivity, kb_weights, block_owner, owner_list):
    shard = image_p.shape
    vmem = pltpu.VMEM
    dma = pltpu.SemaphoreType.DMA
    scratch = [
        vmem((8, 2 * N, 2 * N), BF16),
        vmem((2, 4, N, N), F32),
        vmem((SLOTS * 12, N), F32),
        vmem(shard, F32),
        vmem((NC,) + shard, F32),
        vmem((NT * 8, N), F32),
        vmem((NC, NT, 8, N), F32),
        vmem((8 * N, 2 * N), BF16),
        vmem((2, 8 * N, 2 * N), BF16),
        vmem((4 * N, 8 * N), BF16),
        vmem((8 * N, N), F32),
        vmem((NT, 32, N), F32),
        vmem((8 * N, 4 * N), F32),
        vmem((2, 8 * N, 4 * N), BF16),
        vmem((2, NT // 2, 2, 16, N), F32),
        vmem((2, 4 * N, N), F32),
        vmem((2, 2, 4, 2, 2, 16, N), F32),
        vmem((2, 4, 2, 2, 16, N), F32),
        vmem((2, 4, 2, 2, 16, N), F32),
        vmem((2, 4, 2, 2, 16, N), F32),
        vmem(shard, F32),
        vmem((1, 1, 1, N), F32),
        vmem((1, 1, 1, N), F32),
    ]
    for sizes in ((NC, 8, 4), (NC, NT)):
        scratch += [vmem((len(sizes), 8, N), F32)] + [vmem((n, 8, N), F32) for n in sizes]
    scratch += [dma((n,)) for n in (5, 4, 3, 3)] + [dma(())] * 8
    scratch += [dma((3,))] * 2 + [dma((2,))] * 6 + [dma((3,))] * 5
    step = jax.ShapeDtypeStruct((1, 1, 1, N), F32)
    normal, alpha, beta = pl.pallas_call(
        kernel,
        out_shape=(jax.ShapeDtypeStruct(shard, F32), step, step),
        in_specs=[HBM] * 4 + [SMEM] * 2 + [HBM],
        out_specs=(HBM, HBM, HBM),
        scratch_shapes=scratch,
        compiler_params=pltpu.CompilerParams(
            collective_id=0, has_side_effects=True, vmem_limit_bytes=60 * 2**20
        ),
    )(
        image_p, image_r, sensitivity, kb_weights.reshape(SLOTS * 12, N),
        block_owner, owner_list.transpose(0, 1, 3, 2), jnp.asarray(tables()),
    )
    next_x = image_x + alpha * image_p
    next_r = image_r - alpha * normal
    next_p = next_r + beta * image_p
    return next_x, next_r, next_p


def solution(mesh):
    image = P(None, "tile", "coil", None)
    return jax.shard_map(
        shards,
        mesh=mesh,
        in_specs=(
            image, image, image,
            P("coil", None, "tile", None, None),
            P("tile", None, None, None),
            P("tile"),
            P(None, "tile", None, None),
        ),
        out_specs=(image, image, image),
        check_vma=False,
    )
```

```python
import functools
import math

import jax
import jax.numpy as jnp
import ml_dtypes
import numpy as np
from jax import lax
from jax.experimental import pallas as pl
from jax.experimental.pallas import tpu as pltpu
from jax.sharding import PartitionSpec as P

N = 128
NC = 8
NT = 32
CAP = 4
SLOTS = 32
F32, BF16, I32 = jnp.float32, jnp.bfloat16, jnp.int32
MESH = pl.DeviceIdType.MESH
HBM = pl.BlockSpec(memory_space=pltpu.HBM)
SMEM = pl.BlockSpec(memory_space=pltpu.SMEM)


def tables():
    cells = np.arange(N)
    angle = 2.0 * math.pi / N * ((cells[:, None] * cells[None, :]) % N)
    cos, sin = np.cos(angle) / math.sqrt(N), np.sin(angle) / math.sqrt(N)
    left = np.block([[cos, sin], [-sin, cos]])
    order = [c * N + 4 * t + 2 * p + i for p in range(2) for t in range(NT) for c in range(2) for i in range(2)]
    out = []
    for table in (left, left.T, left[:, order], left[:, order].T):
        table = table.astype(np.float32)
        high = table.astype(ml_dtypes.bfloat16)
        low = (table - high.astype(np.float32)).astype(ml_dtypes.bfloat16)
        out += [high, low]
    return np.stack(out)


def split(x):
    high = x.astype(BF16)
    return high, (x - high.astype(F32)).astype(BF16)


def dot(a, b):
    return jnp.dot(a, b, preferred_element_type=F32)


def dot_t(a, b):
    return lax.dot_general(a, b, (((1,), (1,)), ((), ())), preferred_element_type=F32)


def dot3(a, b):
    return dot(a[0], b[0]) + (dot(a[0], b[1]) + dot(a[1], b[0]))


def kernel(
    p_hbm, r_hbm, s_hbm, kb_hbm, own, offs, tab_hbm,
    normal_hbm, alpha_hbm, beta_hbm,
    tab, smap, kb, rv, pbuf, wsend, wbuf, onehot, pt, pi,
    send1, recv1, boxes, placed, send2, recv2, rs_send, rs_near, rs_sum, rs_recv,
    nv, alphas, betas, ar1, ar1c, ar1z, ar1y, ar2, ar2a, ar2b,
    load_sem, loc_sem, ag_s, ag_r, agf_s, agf_r, w1_s, w1_r, a1_s, a1_r, w2f_s, w2f_r, w2_s, w2_r, a2_s, a2_r,
    rn_s, rn_r, rs_s, rs_r, r1_s, r1_r, r2_s, r2_r, out_sem,
):
    ci, ti = lax.axis_index("coil"), lax.axis_index("tile")
    core, cx = lax.rem(ci, 2), ci // 2
    near = ci + 1 - 2 * core
    z, y = ti // 4, lax.rem(ti, 4)

    loads = [
        pltpu.make_async_copy(src, dst, load_sem.at[i])
        for i, (src, dst) in enumerate(
            [
                (kb_hbm, kb),
                (tab_hbm, tab),
                (s_hbm.at[0], smap),
                (p_hbm, pbuf.at[ci]),
                (r_hbm, rv),
            ]
        )
    ]

    def partner(me, size, i):
        return lax.rem(me + size // 2 + (i + 1) // 2 * (1 - 2 * lax.rem(i, 2)), size)

    def tiles(body, first=0, last=NT - 1):
        def step(i, carry):
            body(partner(z, 8, lax.rem(i, 8)) * 4 + partner(y, 4, i // 8))
            return carry

        lax.fori_loop(first, last, step, 0)

    def ring(me, size, body):
        def step(i, carry):
            body(partner(me, size, i))
            return carry

        lax.fori_loop(0, size - 1, step, 0)

    barrier = pltpu.get_barrier_semaphore()
    tiles(lambda t: pl.semaphore_signal(barrier, inc=1, device_id=(ci, t), device_id_type=MESH))
    ring(ci, NC, lambda c: pl.semaphore_signal(barrier, inc=1, device_id=(c, ti), device_id_type=MESH))

    def greet(count, device):
        def step(i, carry):
            pl.semaphore_signal(barrier, inc=1, device_id=device(i), device_id_type=MESH)
            return carry

        lax.fori_loop(0, count, step, 0)

    for load in loads:
        load.start()

    def push(src, dst, sems, device):
        pltpu.make_async_remote_copy(
            src_ref=src, dst_ref=dst, send_sem=sems[0], recv_sem=sems[1],
            device_id=device, device_id_type=MESH,
        ).start()

    def await_bytes(ref, sem):
        pltpu.make_async_copy(ref, ref, sem).wait()

    over_coil = (NC, ci, lambda i: (partner(ci, NC, i), ti))
    over_z = (8, z, lambda i: (ci, partner(z, 8, i) * 4 + y))
    over_y = (4, y, lambda i: (ci, z * 4 + partner(y, 4, i)))
    over_tile = (32, ti, lambda i: (ci, partner(z, 8, lax.rem(i, 8)) * 4 + partner(y, 4, i // 8)))

    class Sum:
        def __init__(self, part, stages, held, slots, sems):
            self.part, self.stages, self.held, self.slots, self.sems, self.stage = part, stages, held, slots, sems, 0

        def send(self):
            stage = self.stage
            slot, sems = self.slots[stage], (self.sems[0].at[stage], self.sems[1].at[stage])
            self.held[stage] = self.part
            src = self.held.at[stage]
            size, me, device = self.stages[stage]

            def step(i, carry):
                push(src, slot.at[me], sems, device(i))
                return carry

            lax.fori_loop(0, size - 1, step, 0)
            slot[me] = self.part

        def take(self):
            slot = self.slots[self.stage]
            await_bytes(slot.at[pl.ds(0, slot.shape[0] - 1)], self.sems[1].at[self.stage])
            self.part = jnp.sum(slot[...], axis=0)
            self.stage += 1
            return self.part

        def sent(self):
            for stage, slot in enumerate(self.slots):
                await_bytes(slot.at[pl.ds(0, slot.shape[0] - 1)], self.sems[0].at[stage])

    sub = lax.broadcasted_iota(I32, (NT, N), 0)
    lane = lax.broadcasted_iota(I32, (NT, N), 1)
    count = jnp.zeros((NT, N), I32)
    pick = jnp.zeros((NT, N), F32)
    for j in range(SLOTS):
        mine = sub == own[j]
        pick = jnp.where(mine & (lane == j) & (count == cx), 1.0, pick)
        count = jnp.where(mine, count + 1, count)
    pick = pick[:, :SLOTS].astype(BF16)
    loads[0].wait()
    for i in range(8):
        row_a = kb[pl.ds(i // 2, SLOTS, stride=12), :]
        row_b = kb[pl.ds(4 + i, SLOTS, stride=12), :]
        row = jnp.where(core == 0, row_a, row_b)
        high = row.astype(BF16)
        mid, low = split(row - high.astype(F32))
        wsend[pl.ds(i, NT, stride=8), :] = dot(pick, high) + (dot(pick, mid) + dot(pick, low))

    pl.semaphore_wait(barrier, NT - 1 + NC - 1)

    def chip(k):
        return lax.rem(ci + 2 * k, NC)

    loads[3].wait()

    def half_of(c, pair):
        return pbuf.at[c, :, pl.ds(2 * pair, 2)]

    for pair in range(2):
        mine = half_of(ci, pair)
        for k in (2, 1, 3):
            push(mine, mine, (ag_s.at[3 * pair + k - 1], ag_r.at[3 * pair + k - 1]), (chip(k), ti))
        push(mine, mine, (agf_s.at[pair], agf_r.at[pair]), (near, ti))

    def send_weights(first, last):
        tiles(lambda t: push(
            wsend.at[pl.ds(pl.multiple_of(t * 8, 8), 8)], wbuf.at[ci, ti], (w1_s, w1_r), (ci, t)), first, last)

    own_w = pltpu.make_async_copy(wsend.at[pl.ds(pl.multiple_of(ti * 8, 8), 8)], wbuf.at[ci, ti], loc_sem.at[0])
    own_w.start()
    def forward(pair, k):
        came = half_of(chip(4 - k), pair)
        await_bytes(came, ag_r.at[3 * pair + k - 1])
        push(came, came, (agf_s.at[pair], agf_r.at[pair]), (near, ti))

    send_weights(0, 8)
    forward(0, 1)
    forward(0, 3)
    send_weights(8, 12)
    forward(0, 2)
    send_weights(12, 18)
    for k in (1, 3, 2):
        forward(1, k)
    send_weights(18, NT - 1)

    loads[1].wait()
    loads[2].wait()
    left, right = (tab[0], tab[1]), (tab[2], tab[3])

    def place_of(t):
        return pl.ds(pl.multiple_of(t * 16, 16), 16)

    def share_weights():
        own_w.wait()
        await_bytes(wbuf.at[ci, pl.ds(0, NT - 1)], w1_r)
        for k in (2, 1, 3):
            push(wbuf.at[ci], wbuf.at[ci], (w2_s.at[k - 1], w2_r.at[k - 1]), (chip(k), ti))
        push(wbuf.at[ci], wbuf.at[ci], (w2f_s, w2f_r), (near, ti))

    own_1 = []
    for pair in range(2):
        await_bytes(pbuf.at[pl.ds(0, 4), :, pl.ds(0, 2)], agf_r.at[pair])
        parts = []
        for xi in (2 * pair, 2 * pair + 1):
            p_re = pbuf[:, 0, xi].reshape(N, N)
            p_im = pbuf[:, 1, xi].reshape(N, N)
            s_re, s_im = smap[0, xi], smap[1, xi]
            parts.append(jnp.concatenate([s_re * p_re - s_im * p_im, s_re * p_im + s_im * p_re], axis=1))
        along_z = dot3(split(jnp.concatenate(parts, axis=0)), right)
        columns = [
            jnp.concatenate([along_z[i * N : (i + 1) * N, :N], along_z[i * N : (i + 1) * N, N:]], axis=0)
            for i in range(2)
        ]
        along_y = dot3(left, split(jnp.concatenate(columns, axis=1)))
        for i in range(2):
            for c in range(2):
                send1[pair, pl.ds(c * 2 + i, N, stride=4), :] = along_y[c * N : (c + 1) * N, i * N : (i + 1) * N]

        def send_1(t, pair=pair):
            push(
                send1.at[pair, place_of(t)], recv1.at[pair, ti // 2, lax.rem(ti, 2)],
                (a1_s.at[pair], a1_r.at[pair]), (ci, t))

        if pair == 0:
            tiles(send_1, 0, 10)
            share_weights()
            tiles(send_1, 10)
        else:
            tiles(send_1)
        own_1.append(pltpu.make_async_copy(
            send1.at[pair, place_of(ti)], recv1.at[pair, ti // 2, lax.rem(ti, 2)], loc_sem.at[1 + 3 * pair]))
        own_1[pair].start()

    for k in (1, 3, 2):
        came = wbuf.at[chip(4 - k)]
        await_bytes(came, w2_r.at[k - 1])
        push(came, came, (w2f_s, w2f_r), (near, ti))

    sub16 = lax.broadcasted_iota(I32, (16, 2 * N), 0)
    lane16 = lax.broadcasted_iota(I32, (16, 2 * N), 1)
    base16 = (sub16 & 1) * N + ((sub16 >> 1) & 3)

    def mark(h, carry):
        for half in range(2):
            start = jnp.where(sub16 < 8, offs[0, 0, 2 * half, h], offs[0, 0, 2 * half + 1, h])
            hit = jnp.where(lane16 == base16 + start, 1.0, 0.0).astype(BF16)
            onehot[pl.ds(pl.multiple_of(h * 32 + half * 16, 16), 16), :] = hit
        return carry

    lax.fori_loop(0, NT, mark, 0)

    def phases(g, carry):
        rows = pl.ds(pl.multiple_of(g * 256, 256), 256)
        hot = onehot[rows, :]
        for i in range(2):
            pt[i, rows, :] = dot(hot, tab[4 + i]).astype(BF16)
        return carry

    lax.fori_loop(0, 4, phases, 0)
    for i in range(2):
        for g in range(4):
            columns = slice(g * 256, (g + 1) * 256)
            pi[i * 2 * N : (i + 1) * 2 * N, columns] = dot_t(tab[6 + i], onehot[columns, :]).astype(BF16)

    loads[4].wait()
    norm_part = jnp.sum(rv[...].reshape(16, 8, N) * rv[...].reshape(16, 8, N), axis=0)

    for pair in range(2):
        own_1[pair].wait()
        await_bytes(send1.at[pair, pl.ds(0, 16 * (NT - 1))], a1_r.at[pair])
    low = lax.rem(lax.broadcasted_iota(I32, (2 * N, N), 0), 8) < 4
    for e in range(2):
        even = recv1[:, :, 0, e * 8 : (e + 1) * 8, :].reshape(2 * N, N)
        odd = recv1[:, :, 1, e * 8 : (e + 1) * 8, :].reshape(2 * N, N)
        one = jnp.where(low, even, pltpu.roll(odd, 4, 0))
        two = jnp.where(low, pltpu.roll(even, 2 * N - 4, 0), odd)
        boxes[:, 2 * e * N : (2 * e + 2) * N] = dot3((pt[0], pt[1]), split(jnp.concatenate([one, two], axis=1)))

    await_bytes(wbuf.at[pl.ds(0, 4)], w2f_r)
    lane8 = lax.broadcasted_iota(I32, (8, N), 1)
    low8 = lax.broadcasted_iota(I32, (8, N), 0) < 4

    def regrid(g, total):
        spread, pairs, w_xs, starts = [], [], [], []
        for b in range(8):
            h, k = 2 * g + b // 4, b % 4
            w_xs.append(wbuf[2 * k, h])
            w_yz = wbuf[2 * k + 1, h]
            w_z = jnp.where(low8, pltpu.roll(w_yz, 4, 0), w_yz)
            for e in (0, 2):
                pairs.append(jnp.where(low8, w_yz[e : e + 1, :], w_yz[e + 1 : e + 2, :]) * w_z)
            start = offs[2, 0, k, h]
            starts.append(start)
            rows = pl.ds(pl.multiple_of(g * 64 + b * 8, 8), 8)
            moved = jnp.zeros((8, N), F32)
            for e in range(4):
                at = b * 16 + e * 4
                cells = pltpu.roll(boxes[rows, e * N : (e + 1) * N], lax.rem(at + 2 * N - start, N), 1)
                moved = jnp.where((lane8 >= at) & (lane8 < at + 4), cells, moved)
            spread.append(moved)
        pairs = split(jnp.concatenate(pairs, axis=0))
        values = dot3(split(jnp.concatenate(spread, axis=0)), pairs)
        back = []
        for b in range(8):
            value = values[b * 8 : (b + 1) * 8] * w_xs[b]
            value = value + pltpu.roll(value, 4, 0)
            value = value + pltpu.roll(value, 2, 0)
            total = total + value * value
            back.append(value * w_xs[b])
        back = split(jnp.concatenate(back, axis=0))
        cells = dot_t(back[0], pairs[0]) + (dot_t(back[0], pairs[1]) + dot_t(back[1], pairs[0]))
        rows = pl.ds(pl.multiple_of(g * 64, 64), 64)
        for e in range(4):
            parts = []
            for b in range(8):
                at = b * 16 + e * 4
                moved = pltpu.roll(cells[b * 8 : (b + 1) * 8], lax.rem(starts[b] + 2 * N - at, N), 1)
                here = (lane8 >= starts[b]) & (lane8 < starts[b] + 4)
                parts.append(jnp.where(here, moved, 0.0))
            high, low = split(jnp.concatenate(parts, axis=0))
            placed[0, rows, e * N : (e + 1) * N] = high
            placed[1, rows, e * N : (e + 1) * N] = low
        return total

    product_part = lax.fori_loop(0, NT // 2, regrid, jnp.zeros((8, N), F32), unroll=16) * 0.25

    row8 = lax.broadcasted_iota(I32, (8, N), 0)
    norm_row = jnp.sum(norm_part, axis=0, keepdims=True)
    product_row = jnp.sum(product_part, axis=0, keepdims=True)
    both = jnp.where(row8 == 0, norm_row, jnp.where(row8 == 1, product_row, 0.0))
    first_sum = Sum(both, (over_coil, over_z, over_y), ar1, (ar1c, ar1z, ar1y), (r1_s, r1_r))

    owns = []
    for pair in range(2):
        half = jnp.concatenate([pi[pair * N : (pair + 1) * N], pi[(2 + pair) * N : (3 + pair) * N]], axis=0)
        for e in range(2):
            columns = slice(2 * e * N, (2 * e + 2) * N)
            both_terms = dot(half, placed[0, :, columns])
            back = both_terms[:N] + (both_terms[N:] + dot(half[:N], placed[1, :, columns]))
            one, two = back[:, :N], back[:, N:]
            even = jnp.where(low[:N], one, pltpu.roll(two, 4, 0))
            odd = jnp.where(low[:N], pltpu.roll(one, N - 4, 0), two)
            send2[pair, :, 0, e * 8 : (e + 1) * 8, :] = even.reshape(NT // 2, 8, N)
            send2[pair, :, 1, e * 8 : (e + 1) * 8, :] = odd.reshape(NT // 2, 8, N)
        tiles(lambda t, pair=pair: push(
            send2.at[pair, t // 2, lax.rem(t, 2)], recv2.at[pair, place_of(ti)],
            (a2_s.at[pair], a2_r.at[pair]), (ci, t)))
        owns.append(pltpu.make_async_copy(
            send2.at[pair, ti // 2, lax.rem(ti, 2)], recv2.at[pair, place_of(ti)], loc_sem.at[2 + pair]))
        owns[pair].start()
        if pair == 0:
            first_sum.send()
    first_sum.take()
    first_sum.send()

    def spread_sum(pair):
        await_bytes(rs_near.at[pair], rn_r.at[pair])
        rs_sum[pair] = rs_send[core, pair] + rs_near[pair]
        for k in (2, 1, 3):
            to = lax.rem(cx + k, 4)
            push(rs_sum.at[pair, to], rs_recv.at[pair, cx], (rs_s.at[pair], rs_r.at[pair]), (chip(k), ti))
        rs_recv[pair, cx] = rs_sum[pair, cx]

    for pair in range(2):
        owns[pair].wait()
        await_bytes(recv2.at[pair, pl.ds(0, 16 * (NT - 1))], a2_r.at[pair])
        columns = [
            jnp.concatenate([recv2[pair, pl.ds(c * 2 + i, N, stride=4), :] for c in range(2)], axis=0)
            for i in range(2)
        ]
        along_y = dot3(right, split(jnp.concatenate(columns, axis=1)))
        parts = [
            jnp.concatenate([along_y[:N, i * N : (i + 1) * N], along_y[N:, i * N : (i + 1) * N]], axis=1)
            for i in range(2)
        ]
        along_z = dot3(split(jnp.concatenate(parts, axis=0)), left)
        for i in range(2):
            m_re = along_z[i * N : (i + 1) * N, :N]
            m_im = along_z[i * N : (i + 1) * N, N:]
            s_re, s_im = smap[0, 2 * pair + i], smap[1, 2 * pair + i]
            for c, back in enumerate((s_re * m_re + s_im * m_im, s_re * m_im - s_im * m_re)):
                back = back.reshape(4, 2, 16, N)
                for half in range(2):
                    rs_send[half, pair, :, c, i] = back[:, half]
        push(rs_send.at[1 - core, pair], rs_near.at[pair], (rn_s.at[pair], rn_r.at[pair]), (near, ti))
        if pair == 0:
            spread_sum(0)
            first_sum.take()
            first_sum.send()
    spread_sum(1)
    sums = jnp.sum(first_sum.take(), axis=1, keepdims=True)
    norm_now, product = sums[0:1], sums[1:2]
    alpha = norm_now / product
    norm_next = jnp.zeros((8, N), F32)
    for pair in range(2):
        await_bytes(rs_recv.at[pair, pl.ds(0, 3)], rs_r.at[pair])
        normal = jnp.sum(rs_recv[pair], axis=0)
        nv[:, 2 * pair : 2 * pair + 2] = normal
        next_r = rv[:, 2 * pair : 2 * pair + 2].reshape(64, N) - alpha * normal.reshape(64, N)
        norm_next += jnp.sum((next_r * next_r).reshape(8, 8, N), axis=0)
    out_n = pltpu.make_async_copy(nv, normal_hbm, out_sem.at[0])
    out_n.start()

    alphas[...] = jnp.broadcast_to(alpha, (1, N)).reshape(alphas.shape)
    out_a = pltpu.make_async_copy(alphas, alpha_hbm, out_sem.at[1])
    out_a.start()

    last_sum = Sum(norm_next, (over_coil, over_tile), ar2, (ar2a, ar2b), (r2_s, r2_r))
    for _ in range(2):
        last_sum.send()
        sums = last_sum.take()
    sums = jnp.sum(jnp.sum(sums, axis=0, keepdims=True), axis=1, keepdims=True)
    betas[...] = jnp.broadcast_to(sums / norm_now, (1, N)).reshape(betas.shape)
    out_b = pltpu.make_async_copy(betas, beta_hbm, out_sem.at[2])
    out_b.start()

    for i in range(6):
        await_bytes(half_of(0, 0), ag_s.at[i])
    for pair in range(2):
        await_bytes(pbuf.at[pl.ds(0, 4), :, pl.ds(0, 2)], agf_s.at[pair])
        await_bytes(send1.at[pair, pl.ds(0, 16 * (NT - 1))], a1_s.at[pair])
    await_bytes(wbuf.at[0, pl.ds(0, NT - 1)], w1_s)
    for k in range(3):
        await_bytes(wbuf.at[0], w2_s.at[k])
    await_bytes(wbuf.at[pl.ds(0, 4)], w2f_s)
    for pair in range(2):
        await_bytes(recv2.at[pair, pl.ds(0, 16 * (NT - 1))], a2_s.at[pair])
        await_bytes(rs_near.at[pair], rn_s.at[pair])
        await_bytes(rs_recv.at[pair, pl.ds(0, 3)], rs_s.at[pair])
    first_sum.sent()
    last_sum.sent()
    out_n.wait()
    out_a.wait()
    out_b.wait()


def shards(image_p, image_x, image_r, sensitivity, kb_weights, block_owner, owner_list):
    shard = image_p.shape
    vmem = pltpu.VMEM
    dma = pltpu.SemaphoreType.DMA
    scratch = [
        vmem((8, 2 * N, 2 * N), BF16),
        vmem((2, 4, N, N), F32),
        vmem((SLOTS * 12, N), F32),
        vmem(shard, F32),
        vmem((NC,) + shard, F32),
        vmem((NT * 8, N), F32),
        vmem((NC, NT, 8, N), F32),
        vmem((8 * N, 2 * N), BF16),
        vmem((2, 8 * N, 2 * N), BF16),
        vmem((4 * N, 8 * N), BF16),
        vmem((2, 4 * N, N), F32),
        vmem((2, NT // 2, 2, 16, N), F32),
        vmem((8 * N, 4 * N), F32),
        vmem((2, 8 * N, 4 * N), BF16),
        vmem((2, NT // 2, 2, 16, N), F32),
        vmem((2, 4 * N, N), F32),
        vmem((2, 2, 4, 2, 2, 16, N), F32),
        vmem((2, 4, 2, 2, 16, N), F32),
        vmem((2, 4, 2, 2, 16, N), F32),
        vmem((2, 4, 2, 2, 16, N), F32),
        vmem(shard, F32),
        vmem((1, 1, 1, N), F32),
        vmem((1, 1, 1, N), F32),
    ]
    for sizes in ((NC, 8, 4), (NC, NT)):
        scratch += [vmem((len(sizes), 8, N), F32)] + [vmem((n, 8, N), F32) for n in sizes]
    scratch += [dma((n,)) if n else dma(()) for n in (5, 5, 6, 6, 2, 2, 0, 0, 2, 2, 0, 0, 3, 3, 2, 2, 2, 2, 2, 2)]
    scratch += [dma((3,))] * 5
    step = jax.ShapeDtypeStruct((1, 1, 1, N), F32)
    normal, alpha, beta = pl.pallas_call(
        kernel,
        out_shape=(jax.ShapeDtypeStruct(shard, F32), step, step),
        in_specs=[HBM] * 4 + [SMEM] * 2 + [HBM],
        out_specs=(pl.BlockSpec(memory_space=pl.ANY), pl.BlockSpec(memory_space=pl.ANY), pl.BlockSpec(memory_space=pl.ANY)),
        scratch_shapes=scratch,
        compiler_params=pltpu.CompilerParams(
            collective_id=0, has_side_effects=True, vmem_limit_bytes=60 * 2**20
        ),
    )(
        image_p, image_r, sensitivity, kb_weights.reshape(SLOTS * 12, N),
        block_owner, owner_list.transpose(0, 1, 3, 2), jnp.asarray(tables()),
    )
    next_x = image_x + alpha * image_p
    next_r = image_r - alpha * normal
    next_p = next_r + beta * image_p
    return next_x, next_r, next_p


def solution(mesh):
    image = P(None, "tile", "coil", None)
    return jax.shard_map(
        shards,
        mesh=mesh,
        in_specs=(
            image, image, image,
            P("coil", None, "tile", None, None),
            P("tile", None, None, None),
            P("tile"),
            P(None, "tile", None, None),
        ),
        out_specs=(image, image, image),
        check_vma=False,
    )
```
